32 devices in a mesh: gx: 4 (over y, x), gy: 8 (over z, core).
Axes of the slice: x: 2, y: 2, z: 4, core: 2. Of those that a mesh axis runs over, the one named last changes fastest.
Arguments:
- fields: float32 [8, 12, 64, 128], P(None, 'gx', 'gy'), may hold values from -2.1 to 2.1, as said below
- shear_offset: int32 [1], replicated, may hold values from 0 to 63
- row_shift: int32 [12], P('gx'), may hold values from 0 to 63
Outputs:
- advanced: float32 [8, 12, 64, 128], P(None, 'gx', 'gy')
The draws below stay inside these ranges and needn't reach their ends.
Inputs may be any that keep to these rules, and one draw needn't show every extreme that they name: `fields`: component 0 is a density of at least 0.5 and at most 2; component 4 lies between 0 and component 0.
All inputs are finite; a program needn't handle non-finite values.
Results may differ from the reference program's by a relative error of at most 0.00002.
Values sent between devices are 32-bit elements; how exact they have to be, the bound alone decides.
No kernel may reach another device: no remote copies, remote signals or barrier semaphores. Data moves between devices by JAX's collectives and lax.ppermute only.
A program may use at most 64 MiB of HBM per device.

```python
import math
import jax
import jax.numpy as jnp
from jax import lax

CX = 3
NZ = 128
NX = 12
NY = 64
N_GX = 4


def draw_fields(key, part):
    key = jax.random.fold_in(key, 11)
    keys = jax.random.split(key, 4)
    shape = (NX, NY, NZ)
    density = jnp.exp(jax.random.uniform(keys[0], shape, jnp.float32, math.log(0.5), math.log(2.0)))
    momentum = 0.5 * jnp.clip(jax.random.normal(keys[1], (3,) + shape, jnp.float32), -3.0, 3.0)
    magnetic = jnp.clip(0.7 * jax.random.normal(keys[3], (3,) + shape, jnp.float32), -2.1, 2.1)
    dye = jax.random.uniform(keys[2], shape, jnp.float32, 0.0, 1.0) * density
    return jnp.concatenate([density[None], momentum, dye[None], magnetic], axis=0)


def plant(array, own_key, low, top_value):
    spot = [jax.random.randint(jax.random.fold_in(own_key, axis), (), 0, length) for axis, length in enumerate(array.shape)]
    main_axis = array.shape.index(max(array.shape))
    next_to = spot[:main_axis] + [(spot[main_axis] + 1) % array.shape[main_axis]] + spot[main_axis + 1:]
    return array.at[tuple(spot)].set(low).at[tuple(next_to)].set(top_value)


def setup_inputs(seed: int = 0) -> dict:
    splits = jax.random.split(jax.random.key(seed), 4)
    fields = draw_fields(jax.random.fold_in(splits[3], 71), 0)
    shear_offset = jax.random.randint(splits[1], (1,), 0, NY).astype(jnp.int32)
    row_shift = plant(jax.random.randint(splits[2], (NX,), 0, NY), jax.random.fold_in(splits[2], 1), 0, NY - 1).astype(jnp.int32)
    return {"fields": fields, "shear_offset": shear_offset, "row_shift": row_shift}


time_step = 0.2
sound_squared = 1.0
shear_speed = 1.5
sweep_orders = ((0, 1, 2), (1, 2, 0), (2, 0, 1))

def minmod(first_diff, second_diff):
    return jnp.maximum(0.0, jnp.minimum(first_diff, second_diff)) + jnp.minimum(0.0, jnp.maximum(first_diff, second_diff))

def edge_states(values, direction):
    if direction == 2:
        lower_cell = jnp.roll(values, 1, axis=2)
        upper_cell = jnp.roll(values, -1, axis=2)
        gradient = minmod(values - lower_cell, upper_cell - values)
        left_face = jnp.roll(values + 0.5 * gradient, 1, axis=2)
        right_face = values - 0.5 * gradient
        return (left_face, right_face)
    extent = values.shape[direction]
    lower_cell = lax.slice_in_dim(values, 0, extent - 2, axis=direction)
    middle = lax.slice_in_dim(values, 1, extent - 1, axis=direction)
    upper_cell = lax.slice_in_dim(values, 2, extent, axis=direction)
    gradient = minmod(middle - lower_cell, upper_cell - middle)
    left_face = lax.slice_in_dim(middle + 0.5 * gradient, 0, extent - 3, axis=direction)
    right_face = lax.slice_in_dim(middle - 0.5 * gradient, 1, extent - 2, axis=direction)
    return (left_face, right_face)

def side_terms(primitive, normal_field):
    density, normal_vel, tang_one, tang_two, field_one, field_two, fraction = primitive
    pressure = sound_squared * density + 0.5 * (normal_field * normal_field + field_one * field_one + field_two * field_two)
    fluxes = (density * normal_vel, density * normal_vel * normal_vel + pressure - normal_field * normal_field, density * normal_vel * tang_one - normal_field * field_one, density * normal_vel * tang_two - normal_field * field_two, normal_vel * field_one - tang_one * normal_field, normal_vel * field_two - tang_two * normal_field, density * fraction * normal_vel)
    conserved = (density, density * normal_vel, density * tang_one, density * tang_two, field_one, field_two, density * fraction)
    normal_alfven = normal_field * normal_field / density
    tangent_alfven = (field_one * field_one + field_two * field_two) / density
    spread = (sound_squared - normal_alfven) ** 2 + tangent_alfven * tangent_alfven + 2.0 * tangent_alfven * (sound_squared + normal_alfven)
    fast_speed = jnp.sqrt(0.5 * (sound_squared + normal_alfven + tangent_alfven + jnp.sqrt(spread)))
    return (fluxes, conserved, normal_vel - fast_speed, normal_vel + fast_speed)

def hll_flux(left_side, right_side, normal_field):
    flux_left_all, cons_left_all, low_left, high_left = side_terms(left_side, normal_field)
    flux_right_all, cons_right_all, low_right, high_right = side_terms(right_side, normal_field)
    lower_speed = jnp.minimum(jnp.minimum(low_left, low_right), 0.0)
    upper_speed = jnp.maximum(jnp.maximum(high_left, high_right), 0.0)
    inverse_gap = 1.0 / (upper_speed - lower_speed)
    return tuple(((upper_speed * flux_left - lower_speed * flux_right + lower_speed * upper_speed * (cons_right - cons_left)) * inverse_gap for flux_left, flux_right, cons_left, cons_right in zip(flux_left_all, flux_right_all, cons_left_all, cons_right_all)))

def sweep(density, velocity, fraction, centres, faces, direction):
    normal_axis, first_axis, second_axis = sweep_orders[direction]
    states = (density, velocity[normal_axis], velocity[first_axis], velocity[second_axis], centres[first_axis], centres[second_axis], fraction)
    face_pairs = [edge_states(values, direction) for values in states]
    left_side = tuple((pair_item[0] for pair_item in face_pairs))
    right_side = tuple((pair_item[1] for pair_item in face_pairs))
    if direction == 2:
        normal_field = faces[2]
    else:
        extent = faces[direction].shape[direction]
        normal_field = lax.slice_in_dim(faces[direction], 2, extent - 1, axis=direction)
    return hll_flux(left_side, right_side, normal_field)

def momentum_parts(fluxes, direction):
    normal_axis, first_axis, second_axis = sweep_orders[direction]
    parts = [fluxes[1], fluxes[1], fluxes[1]]
    parts[normal_axis] = fluxes[1]
    parts[first_axis] = fluxes[2]
    parts[second_axis] = fluxes[3]
    return parts

def predict(padded):
    cells_x = padded.shape[1] - 6
    cells_y = padded.shape[2] - 6
    face_x, face_y, face_z = (padded[5], padded[6], padded[7])
    centres = ((0.5 * (face_x[:-1] + face_x[1:]))[:, :-1], (0.5 * (face_y[:, :-1] + face_y[:, 1:]))[:-1], (0.5 * (face_z + jnp.roll(face_z, -1, axis=2)))[:-1, :-1])
    density = padded[0][:-1, :-1]
    inverse = 1.0 / density
    velocity = tuple((padded[component][:-1, :-1] * inverse for component in (1, 2, 3)))
    fraction = padded[4][:-1, :-1] * inverse
    faces = (face_x[:-1, :-1], face_y[:-1, :-1], face_z[:-1, :-1])
    flux_x = sweep(density, velocity, fraction, centres, faces, 0)
    flux_y = sweep(density, velocity, fraction, centres, faces, 1)
    flux_z = sweep(density, velocity, fraction, centres, faces, 2)

    def diverge(along_x, along_y, along_z):
        return along_x[2:cells_x + 2, 3:cells_y + 3] - along_x[1:cells_x + 1, 3:cells_y + 3] + along_y[3:cells_x + 3, 2:cells_y + 2] - along_y[3:cells_x + 3, 1:cells_y + 1] + (jnp.roll(along_z, -1, axis=2) - along_z)[3:cells_x + 3, 3:cells_y + 3]

    def own_cells(component):
        return padded[component][3:cells_x + 3, 3:cells_y + 3]
    parts_x = momentum_parts(flux_x, 0)
    parts_y = momentum_parts(flux_y, 1)
    parts_z = momentum_parts(flux_z, 2)
    new_density = own_cells(0) - time_step * diverge(flux_x[0], flux_y[0], flux_z[0])
    new_momentum = [own_cells(1 + component) - time_step * diverge(parts_x[component], parts_y[component], parts_z[component]) for component in range(3)]
    new_dye = own_cells(4) - time_step * diverge(flux_x[6], flux_y[6], flux_z[6])
    edge_z = 0.25 * (-flux_x[4][1:cells_x + 2, 3:cells_y + 4] - flux_x[4][1:cells_x + 2, 2:cells_y + 3] + flux_y[5][3:cells_x + 4, 1:cells_y + 2] + flux_y[5][2:cells_x + 3, 1:cells_y + 2])
    across_x = flux_x[5][1:cells_x + 2, 3:cells_y + 3]
    edge_y = 0.25 * (across_x + jnp.roll(across_x, 1, axis=2) - flux_z[4][3:cells_x + 4, 3:cells_y + 3] - flux_z[4][2:cells_x + 3, 3:cells_y + 3])
    across_y = flux_y[4][3:cells_x + 3, 1:cells_y + 2]
    edge_x = 0.25 * (-across_y - jnp.roll(across_y, 1, axis=2) + flux_z[5][3:cells_x + 3, 3:cells_y + 4] + flux_z[5][3:cells_x + 3, 2:cells_y + 3])
    low_y = edge_y[0:cells_x]
    new_bx = own_cells(5) - time_step * (edge_z[0:cells_x, 1:cells_y + 1] - edge_z[0:cells_x, 0:cells_y]) + time_step * (jnp.roll(low_y, -1, axis=2) - low_y)
    low_x = edge_x[:, 0:cells_y]
    new_by = own_cells(6) - time_step * (jnp.roll(low_x, -1, axis=2) - low_x) + time_step * (edge_z[1:cells_x + 1, 0:cells_y] - edge_z[0:cells_x, 0:cells_y])
    new_bz = own_cells(7) - time_step * (edge_y[1:cells_x + 1] - edge_y[0:cells_x]) + time_step * (edge_x[:, 1:cells_y + 1] - edge_x[:, 0:cells_y])
    return jnp.stack([new_density] + new_momentum + [new_dye, new_bx, new_by, new_bz])

def reference(fields, shear_offset, row_shift):
    offset = shear_offset[0]
    low_ghost = jnp.roll(fields[:, NX - 3:], -offset, axis=2)
    low_ghost = low_ghost.at[2].add(shear_speed * low_ghost[0])
    high_ghost = jnp.roll(fields[:, :3], offset, axis=2)
    high_ghost = high_ghost.at[2].add(-shear_speed * high_ghost[0])
    extended = jnp.concatenate([low_ghost, fields, high_ghost], axis=1)
    extended = jnp.concatenate([extended[:, :, NY - 3:], extended, extended[:, :, :3]], axis=2)

    def one_block(block_index):
        window = lax.dynamic_slice_in_dim(extended, block_index * CX, CX + 6, axis=1)
        return predict(window)
    blocks = lax.map(one_block, jnp.arange(N_GX, dtype=jnp.int32))
    updated = jnp.moveaxis(blocks, 0, 1).reshape(8, NX, NY, NZ)

    def advect_row(row_block, amount):
        return jnp.roll(row_block, amount, axis=1)
    return jax.vmap(advect_row, in_axes=(1, 0), out_axes=1)(updated, row_shift)
```

```python
import functools
import jax
import jax.numpy as jnp
from jax import lax
from jax.experimental import pallas as pl
from jax.experimental.pallas import tpu as pltpu
from jax.sharding import PartitionSpec as P

time_step = 0.2
sound_squared = 1.0
shear_speed = 1.5
sweep_orders = ((0, 1, 2), (1, 2, 0), (2, 0, 1))


def remainder(value, by):
    return value & (by - 1) if by & (by - 1) == 0 else lax.rem(value, by)


def quotient(value, by):
    return value >> (by.bit_length() - 1) if by & (by - 1) == 0 else lax.div(value, by)


def minmod(first_diff, second_diff):
    return jnp.maximum(0.0, jnp.minimum(first_diff, second_diff)) + jnp.minimum(
        0.0, jnp.maximum(first_diff, second_diff)
    )


def shift(values, by, axis):
    return pltpu.roll(values, by % values.shape[axis], axis=axis)


def side_terms(state, normal_field):
    density, normal_vel, tang_one, tang_two, field_one, field_two, fraction = state
    normal_square = normal_field * normal_field
    tangent_square = field_one * field_one + field_two * field_two
    mass_flux = density * normal_vel
    dye = density * fraction
    fluxes = (
        mass_flux,
        mass_flux * normal_vel + sound_squared * density + 0.5 * (tangent_square - normal_square),
        mass_flux * tang_one - normal_field * field_one,
        mass_flux * tang_two - normal_field * field_two,
        normal_vel * field_one - tang_one * normal_field,
        normal_vel * field_two - tang_two * normal_field,
        dye * normal_vel,
    )
    conserved = (
        density,
        mass_flux,
        density * tang_one,
        density * tang_two,
        field_one,
        field_two,
        dye,
    )
    inverse = 1.0 / density
    normal_alfven = normal_square * inverse
    tangent_alfven = tangent_square * inverse
    apart = sound_squared - normal_alfven
    spread = (
        apart * apart
        + tangent_alfven * tangent_alfven
        + 2.0 * tangent_alfven * (sound_squared + normal_alfven)
    )
    fast_speed = jnp.sqrt(0.5 * (sound_squared + normal_alfven + tangent_alfven + jnp.sqrt(spread)))
    return (fluxes, conserved, normal_vel - fast_speed, normal_vel + fast_speed)


def hll_flux(left_side, right_side, normal_field):
    flux_left_all, cons_left_all, low_left, high_left = side_terms(left_side, normal_field)
    flux_right_all, cons_right_all, low_right, high_right = side_terms(right_side, normal_field)
    lower_speed = jnp.minimum(jnp.minimum(low_left, low_right), 0.0)
    upper_speed = jnp.maximum(jnp.maximum(high_left, high_right), 0.0)
    inverse_gap = 1.0 / (upper_speed - lower_speed)
    upper = upper_speed * inverse_gap
    lower = lower_speed * inverse_gap
    product = lower_speed * upper
    return tuple(
        upper * flux_left - lower * flux_right + product * (cons_right - cons_left)
        for flux_left, flux_right, cons_left, cons_right in zip(
            flux_left_all, flux_right_all, cons_left_all, cons_right_all
        )
    )


def low_windows(cells_x):
    return [(i, i + k) for i in range(cells_x) for k in (-2, -1) if i + k < 0]


def high_windows(cells_x):
    return [(i, i + k) for i in range(cells_x) for k in (1, 2) if i + k >= cells_x]


def tile_reader(source, start, length, first_tile, tiles):
    cells_y, cells_z = source.shape[3:]
    blocks = length // cells_y
    block = quotient(start, cells_y)
    turn = remainder(start, cells_y)
    inside = lax.broadcasted_iota(jnp.int32, (cells_y, cells_z), 0) < cells_y - turn
    places = [remainder(block + first_tile + k + blocks, blocks) for k in range(tiles + 1)]

    def read(component, row):
        turned = [pltpu.roll(source[place, component, row], cells_y - turn, axis=0) for place in places]
        return [jnp.where(inside, turned[k], turned[k + 1]) for k in range(tiles)]

    return read


class Row:
    def __init__(self, known):
        self.known = dict(known)

    def get(self, *key):
        if key not in self.known:
            getattr(self, "make_" + key[0])(*key[1:-1])
        return self.known[key]

    def all(self, *key):
        return tuple(self.get(*key, item) for item in range(7))

    def put(self, key, values):
        for item, value in enumerate(values):
            self.known[key + (item,)] = value

    def make_cell(self, k):
        raw = [self.get("raw", k, component) for component in range(8)]
        inverse = 1.0 / raw[0]
        self.put(
            ("cell", k),
            (
                raw[0],
                raw[1] * inverse,
                raw[2] * inverse,
                raw[3] * inverse,
                0.5 * (raw[6] + shift(raw[6], -1, 0)),
                0.5 * (raw[7] + shift(raw[7], -1, 1)),
                raw[4] * inverse,
            ),
        )

    def make_centre_x(self, k):
        self.put(("centre_x", k), [0.5 * (self.get("raw", k, 5) + self.get("raw", k + 1, 5))])

    def make_slope(self, k):
        three = [self.all("cell", k + step) for step in (-1, 0, 1)]
        self.put(("slope", k), [0.5 * minmod(h - b, a - h) for b, h, a in zip(*three)])

    def make_along_0(self, face):
        left = [w + s for w, s in zip(self.all("cell", face + 1), self.all("slope", face + 1))]
        right = [w - s for w, s in zip(self.all("cell", face + 2), self.all("slope", face + 2))]
        self.put(("along_0", face), hll_flux(left, right, self.get("raw", face + 2, 5)))

    def sweep(self, k, direction, axis):
        density, vel_x, vel_y, vel_z, centre_y, centre_z, fraction = self.all("cell", k)
        velocity = (vel_x, vel_y, vel_z)
        centres = (self.get("centre_x", k, 0), centre_y, centre_z)
        normal_axis, first_axis, second_axis = sweep_orders[direction]
        states = (
            density,
            velocity[normal_axis],
            velocity[first_axis],
            velocity[second_axis],
            centres[first_axis],
            centres[second_axis],
            fraction,
        )
        left, right = [], []
        for w in states:
            half = 0.5 * minmod(w - shift(w, 1, axis), shift(w, -1, axis) - w)
            left.append(shift(w + half, 1, axis))
            right.append(w - half)
        return hll_flux(left, right, self.get("raw", k, 5 + direction))

    def make_along_1(self, k):
        self.put(("along_1", k), self.sweep(k, 1, 0))

    def make_along_2(self, k):
        self.put(("along_2", k), self.sweep(k, 2, 1))

    def make_out(self):
        along_x = [self.all("along_0", face) for face in range(2)]
        along_y, along_z = self.all("along_1", 2), self.all("along_2", 2)
        edge_z = [
            0.25
            * (
                self.get("along_1", face + 2, 5)
                + self.get("along_1", face + 1, 5)
                - along_x[face][4]
                - shift(along_x[face][4], 1, 0)
            )
            for face in range(2)
        ]
        edge_y = [
            0.25
            * (
                along_x[face][5]
                + shift(along_x[face][5], 1, 1)
                - self.get("along_2", face + 2, 4)
                - self.get("along_2", face + 1, 4)
            )
            for face in range(2)
        ]
        edge_x = 0.25 * (
            along_z[5] + shift(along_z[5], 1, 0) - along_y[4] - shift(along_y[4], 1, 1)
        )
        own = [self.get("raw", 2, component) for component in range(8)]
        places = ((1, 2, 3), (3, 1, 2), (2, 3, 1))
        values = []
        for component in range(5):
            if component == 0:
                slots = (0, 0, 0)
            elif component == 4:
                slots = (6, 6, 6)
            else:
                slots = tuple(places[d][component - 1] for d in range(3))
            through_y, through_z = along_y[slots[1]], along_z[slots[2]]
            total = (
                along_x[1][slots[0]]
                - along_x[0][slots[0]]
                + shift(through_y, -1, 0)
                - through_y
                + shift(through_z, -1, 1)
                - through_z
            )
            values.append(own[component] - time_step * total)
        values.append(
            own[5]
            - time_step * (shift(edge_z[0], -1, 0) - edge_z[0])
            + time_step * (shift(edge_y[0], -1, 1) - edge_y[0])
        )
        values.append(
            own[6]
            - time_step * (shift(edge_x, -1, 1) - edge_x)
            + time_step * (edge_z[1] - edge_z[0])
        )
        values.append(
            own[7]
            - time_step * (edge_y[1] - edge_y[0])
            + time_step * (shift(edge_x, -1, 0) - edge_x)
        )
        self.put(("out",), values)


def message(wanted):
    mains, slots = [], []
    for row, radial in wanted:
        k = radial - row + 2
        if k in (1, 3):
            mains += [(row, "raw", k, component) for component in range(8)]
            slots += [[(row, "raw", k, component)] for component in (0, 1, 2, 5, 6, 7)]
        else:
            mains += [(row, "cell", k, item) for item in range(7)]
            slots += [[(row, "cell", k, item) for item in pair] for pair in ((0, 1), (2, 4), (5,))]
            if k == 4:
                mains.append((row, "raw", k, 5))
                slots.append([(row, "raw", k, 5)])
    return mains, slots


def message_tiles(wanted):
    mains, slots = message(wanted)
    return len(mains) + (len(slots) + 1) // 2


def pack(out, wanted, values):
    mains, slots = message(wanted)
    sub = lax.broadcasted_iota(jnp.int32, out.shape[1:], 0)
    rows = out.shape[1]
    for at, (row, *key) in enumerate(mains):
        out[at] = values[row].get(*key)[:rows]

    def slot(keys):
        around = [values[row].get(*key)[rows:] for row, *key in keys]
        first = around[0]
        tile = jnp.where(sub < 2, first, shift(first, 4, 0))
        if len(around) == 2:
            second = around[1]
            tile = jnp.where(sub == 1, shift(second, 1, 0), tile)
            tile = jnp.where(sub == 2, shift(second, 3, 0), tile)
        return tile

    for at in range(0, len(slots), 2):
        tile = slot(slots[at])
        if at + 1 < len(slots):
            tile = jnp.where(sub < 4, tile, shift(slot(slots[at + 1]), 4, 0))
        out[len(mains) + at // 2] = tile


def unpack(source, wanted, known):
    mains, slots = message(wanted)
    sub = lax.broadcasted_iota(jnp.int32, source.shape[1:], 0)
    edges = {}
    for at, keys in enumerate(slots):
        tile = source[len(mains) + at // 2]
        turned = shift(tile, 4, 0)
        one, two = (tile, turned) if at % 2 == 0 else (turned, tile)
        around = jnp.where(sub < 4, one, two)
        edges[keys[0]] = around
        if len(keys) == 2:
            edges[keys[1]] = jnp.where(sub < 4, shift(around, -1, 0), shift(around, 1, 0))
    for at, key in enumerate(mains):
        main = source[at]
        known[key[0]][key[1:]] = jnp.concatenate([main, edges.get(key, main)], axis=0)


def windows_call(near, far, received, swapped, offset):
    count = len(near)
    parts, cells_x, cells_y, cells_z = near[0].shape
    blocks = 2 * count
    length = blocks * cells_y
    lows, highs = low_windows(cells_x), high_windows(cells_x)

    def body(offset, received, swapped, *refs):
        ins, whole, outs = refs[:blocks], refs[blocks], refs[blocks + 1 : -2]
        shifts, sems = refs[-2:]
        copies = [
            pltpu.make_async_copy(source, shifts.at[at], sems.at[at])
            for at, source in enumerate((received, swapped))
        ]
        for copy in copies:
            copy.start()
        place_x, place_y = lax.axis_index("gx"), lax.axis_index("gy")
        last = lax.axis_size("gx") - 1
        for side in range(2):
            for step in range(count):
                block = ins[side * count + step]
                place = remainder((place_y ^ side) - 2 * step + blocks, blocks)
                if side == 0 and step == 0:
                    whole[place, : parts // 2] = block[parts // 2 :]
                    whole[place, parts // 2 :] = block[: parts // 2]
                else:
                    whole[place] = block[...]
        sub = lax.broadcasted_iota(jnp.int32, (cells_y, cells_z), 0)
        for copy in copies:
            copy.wait()
        here = remainder(place_x + place_y, 2) == 0
        above, below = (
            [jnp.where(here, shifts[one, i], shifts[1 - one, i]) for i in range(cells_x)]
            for one in range(2)
        )
        for out, shift_by, wanted, end, sign, turn in (
            (outs[0], above, lows, last, 1, cells_x),
            (outs[1], below, highs, 0, -1, -cells_x),
        ):
            at_end = place_x == end
            away = jnp.where(at_end, sign * offset[0], 0)
            boost = jnp.where(at_end, sign * shear_speed, 0.0)
            known = {}
            for row, radial in wanted:
                start = remainder(place_y * cells_y - shift_by[row] + away + 2 * length, length)
                read = tile_reader(whole, start, length, -1, 3)
                raw = []
                for component in range(parts):
                    before, main, after = read(component, radial + turn)
                    raw.append(jnp.concatenate([main, jnp.where(sub < 4, after, before)], axis=0))
                raw[2] = raw[2] + boost * raw[0]
                for component in range(parts):
                    known.setdefault(row, {})["raw", radial - row + 2, component] = raw[component]
            pack(out, wanted, {row: Row(found) for row, found in known.items()})

    vmem = pl.BlockSpec(memory_space=pltpu.VMEM)
    smem = pl.BlockSpec(memory_space=pltpu.SMEM)
    return pl.pallas_call(
        body,
        out_shape=[jax.ShapeDtypeStruct((blocks, parts, cells_x, cells_y, cells_z), jnp.float32)]
        + [
            jax.ShapeDtypeStruct((message_tiles(wanted), cells_y, cells_z), jnp.float32)
            for wanted in (lows, highs)
        ],
        in_specs=[smem] + [vmem] * (2 + blocks),
        out_specs=[vmem] * 3,
        scratch_shapes=[pltpu.SMEM((2, cells_x), jnp.int32), pltpu.SemaphoreType.DMA((2,))],
        compiler_params=pltpu.CompilerParams(vmem_limit_bytes=32 * 1024 * 1024),
        name="windows",
    )(offset, received, swapped, *near, *far)


def reads(key):
    name, *rest = key
    if name == "out":
        found = [("raw", 2, component) for component in range(8)]
        found += [("along_0", face, item) for face in range(2) for item in range(7)]
        found += [(along, 2, item) for along in ("along_1", "along_2") for item in range(7)]
        return found + [(along, k, item) for k in (1, 3) for along, item in (("along_1", 5), ("along_2", 4))]
    if name == "cell":
        return [("raw", rest[0], component) for component in range(8)]
    if name == "centre_x":
        return [("raw", rest[0], 5), ("raw", rest[0] + 1, 5)]
    if name == "slope":
        return [("cell", rest[0] + step, rest[1]) for step in (-1, 0, 1)]
    if name == "along_0":
        cells = [rest[0] + 1, rest[0] + 2]
        found = [(of, k, item) for k in cells for of in ("cell", "slope") for item in range(7)]
        return found + [("raw", cells[1], 5)]
    found = [("cell", rest[0], item) for item in range(7)] + [("centre_x", rest[0], 0)]
    return found + [("raw", rest[0], {"along_1": 6, "along_2": 7}[name])]


def handed_on(cells_x):
    plans = []
    for row in range(cells_x):

        def stage_of_ghost(k):
            return 0 if 0 <= row + k - 2 < cells_x else 1 if row + k - 2 >= cells_x else 2

        stages, readers = {}, {}

        def stage(key):
            if key not in stages:
                given = key[0] == "raw" or (key[0] == "cell" and key[1] in (0, 4) and stage_of_ghost(key[1]))
                if given:
                    stages[key] = stage_of_ghost(key[1])
                else:
                    stages[key] = max(stage(found) for found in reads(key))
                    for found in reads(key):
                        readers.setdefault(found, []).append(key)
            return stages[key]

        ends = [("out", component) for component in range(8)]
        for key in ends:
            stage(key)
        plans.append(
            [
                [
                    key
                    for key, at in stages.items()
                    if at == level
                    and (key in ends or any(stages[reader] > level for reader in readers[key]))
                ]
                for level in range(2)
            ]
        )
    return plans


def own_windows(wholes, row, row_shift, known):
    _, parts, cells_x, cells_y, cells_z = wholes.shape
    length = wholes.shape[0] * cells_y
    sub = lax.broadcasted_iota(jnp.int32, (cells_y, cells_z), 0)
    start = remainder(lax.axis_index("gy") * cells_y - row_shift[row] + length, length)
    read = tile_reader(wholes, start, length, -1, 3)
    for k in range(5):
        radial = row + k - 2
        if 0 <= radial < cells_x:
            for component in range(parts):
                before, main, after = read(component, radial)
                around = jnp.where(sub < 4, after, before)
                known["raw", k, component] = jnp.concatenate([main, around], axis=0)


def inner_call(whole, row_shift):
    _, _, cells_x, cells_y, cells_z = whole.shape
    plans = handed_on(cells_x)

    def body(row_shift, whole, out):
        at = 0
        for row in range(cells_x):
            known = {}
            own_windows(whole, row, row_shift, known)
            values = Row(known)
            for key in plans[row][0]:
                out[at] = values.get(*key)
                at += 1

    vmem = pl.BlockSpec(memory_space=pltpu.VMEM)
    total = sum(len(plan[0]) for plan in plans)
    return pl.pallas_call(
        body,
        out_shape=jax.ShapeDtypeStruct((total, 2 * cells_y, cells_z), jnp.float32),
        in_specs=[pl.BlockSpec(memory_space=pltpu.SMEM), vmem],
        out_specs=vmem,
        compiler_params=pltpu.CompilerParams(vmem_limit_bytes=32 * 1024 * 1024),
        cost_estimate=pl.CostEstimate(flops=10**7, bytes_accessed=10**6, transcendentals=10**5),
        name="inner",
    )(row_shift, whole)


def load_stage(plans, level, ref, known):
    at = 0
    for row, plan in enumerate(plans):
        for key in plan[level]:
            known[row][key] = ref[at]
            at += 1


def middle_call(inner, from_above, cells_x):
    plans = handed_on(cells_x)

    def body(inner, from_above, out):
        known = [{} for _ in range(cells_x)]
        load_stage(plans, 0, inner, known)
        unpack(from_above, high_windows(cells_x), known)
        at = 0
        for row in range(cells_x):
            values = Row(known[row])
            for key in plans[row][1]:
                out[at] = values.get(*key)
                at += 1

    vmem = pl.BlockSpec(memory_space=pltpu.VMEM)
    total = sum(len(plan[1]) for plan in plans)
    return pl.pallas_call(
        body,
        out_shape=jax.ShapeDtypeStruct((total,) + inner.shape[1:], jnp.float32),
        in_specs=[vmem] * 2,
        out_specs=vmem,
        compiler_params=pltpu.CompilerParams(vmem_limit_bytes=32 * 1024 * 1024),
        cost_estimate=pl.CostEstimate(flops=10**6, bytes_accessed=10**6, transcendentals=10**4),
        name="middle",
    )(inner, from_above)


def outer_call(inner, middle, from_below, cells_x, parts):
    cells_y, cells_z = inner.shape[1] // 2, inner.shape[2]
    plans = handed_on(cells_x)

    def body(inner, middle, from_below, out):
        known = [{} for _ in range(cells_x)]
        load_stage(plans, 0, inner, known)
        load_stage(plans, 1, middle, known)
        unpack(from_below, low_windows(cells_x), known)
        for row in range(cells_x):
            values = Row(known[row])
            for component in range(parts):
                out[component, row] = values.get("out", component)[0:cells_y]

    vmem = pl.BlockSpec(memory_space=pltpu.VMEM)
    return pl.pallas_call(
        body,
        out_shape=jax.ShapeDtypeStruct((parts, cells_x, cells_y, cells_z), jnp.float32),
        in_specs=[vmem] * 3,
        out_specs=vmem,
        compiler_params=pltpu.CompilerParams(vmem_limit_bytes=32 * 1024 * 1024),
        name="outer",
    )(inner, middle, from_below)


def on_device(fields, shear_offset, row_shift):
    count_x, count_y = lax.axis_size("gx"), lax.axis_size("gy")
    upward = [(i, (i + 1) % count_x) for i in range(count_x)]
    downward = [(target, source) for source, target in upward]

    def other_core(values):
        return lax.ppermute(values, "gy", [(i, i ^ 1) for i in range(count_y)])

    own = jnp.roll(fields, fields.shape[0] // 2, axis=0)
    meet = []
    for x in range(count_x):
        for y in range(count_y):
            other = (x + 1 if (x + y) % 2 == 0 else x - 1) % count_x
            meet.append((x * count_y + y, other * count_y + y))
    received = lax.ppermute(row_shift, ("gx", "gy"), meet)
    swapped = other_core(received)
    near = [fields] + [
        lax.ppermute(fields, "gy", [(i, (i + step) % count_y) for i in range(count_y)])
        for step in range(2, count_y, 2)
    ]
    passed_on = list(near)
    middle = len(near) // 2
    passed_on[middle], received, swapped = lax.optimization_barrier(
        (near[middle], received, swapped)
    )
    far = [other_core(values) for values in passed_on]
    near[0] = own
    whole, to_above, to_below = windows_call(near, far, received, swapped, shear_offset)
    from_below = lax.ppermute(to_above, "gx", upward)
    from_above = lax.ppermute(to_below, "gx", downward)
    inner = inner_call(whole, row_shift)
    middle = middle_call(inner, from_above, fields.shape[1])
    return outer_call(inner, middle, from_below, fields.shape[1], fields.shape[0])


def solution(mesh):
    placed = (P(None, "gx", "gy", None), P(), P("gx"))
    return jax.shard_map(
        on_device, mesh=mesh, in_specs=placed, out_specs=P(None, "gx", "gy", None), check_vma=False
    )
```

```python
import functools
import jax
import jax.numpy as jnp
from jax import lax
from jax.experimental import pallas as pl
from jax.experimental.pallas import tpu as pltpu
from jax.sharding import PartitionSpec as P

time_step = 0.2
sound_squared = 1.0
shear_speed = 1.5
sweep_orders = ((0, 1, 2), (1, 2, 0), (2, 0, 1))


def remainder(value, by):
    return value & (by - 1) if by & (by - 1) == 0 else lax.rem(value, by)


def quotient(value, by):
    return value >> (by.bit_length() - 1) if by & (by - 1) == 0 else lax.div(value, by)


def minmod(first_diff, second_diff):
    return jnp.maximum(0.0, jnp.minimum(first_diff, second_diff)) + jnp.minimum(
        0.0, jnp.maximum(first_diff, second_diff)
    )


def shift(values, by, axis):
    return pltpu.roll(values, by % values.shape[axis], axis=axis)


def side_terms(state, normal_field):
    density, normal_vel, tang_one, tang_two, field_one, field_two, fraction = state
    normal_square = normal_field * normal_field
    tangent_square = field_one * field_one + field_two * field_two
    mass_flux = density * normal_vel
    dye = density * fraction
    fluxes = (
        mass_flux,
        mass_flux * normal_vel + sound_squared * density + 0.5 * (tangent_square - normal_square),
        mass_flux * tang_one - normal_field * field_one,
        mass_flux * tang_two - normal_field * field_two,
        normal_vel * field_one - tang_one * normal_field,
        normal_vel * field_two - tang_two * normal_field,
        dye * normal_vel,
    )
    conserved = (
        density,
        mass_flux,
        density * tang_one,
        density * tang_two,
        field_one,
        field_two,
        dye,
    )
    inverse = 1.0 / density
    normal_alfven = normal_square * inverse
    tangent_alfven = tangent_square * inverse
    apart = sound_squared - normal_alfven
    spread = (
        apart * apart
        + tangent_alfven * tangent_alfven
        + 2.0 * tangent_alfven * (sound_squared + normal_alfven)
    )
    fast_speed = jnp.sqrt(0.5 * (sound_squared + normal_alfven + tangent_alfven + jnp.sqrt(spread)))
    return (fluxes, conserved, normal_vel - fast_speed, normal_vel + fast_speed)


def hll_flux(left_side, right_side, normal_field):
    flux_left_all, cons_left_all, low_left, high_left = side_terms(left_side, normal_field)
    flux_right_all, cons_right_all, low_right, high_right = side_terms(right_side, normal_field)
    lower_speed = jnp.minimum(jnp.minimum(low_left, low_right), 0.0)
    upper_speed = jnp.maximum(jnp.maximum(high_left, high_right), 0.0)
    inverse_gap = 1.0 / (upper_speed - lower_speed)
    upper = upper_speed * inverse_gap
    lower = lower_speed * inverse_gap
    product = lower_speed * upper
    return tuple(
        upper * flux_left - lower * flux_right + product * (cons_right - cons_left)
        for flux_left, flux_right, cons_left, cons_right in zip(
            flux_left_all, flux_right_all, cons_left_all, cons_right_all
        )
    )


def low_windows(cells_x):
    return [(i, i + k) for i in range(cells_x) for k in (-2, -1) if i + k < 0]


def high_windows(cells_x):
    return [(i, i + k) for i in range(cells_x) for k in (1, 2) if i + k >= cells_x]


def tile_reader(source, start, length, first_tile, tiles):
    cells_y, cells_z = source.shape[3:]
    blocks = length // cells_y
    block = quotient(start, cells_y)
    turn = remainder(start, cells_y)
    inside = lax.broadcasted_iota(jnp.int32, (cells_y, cells_z), 0) < cells_y - turn
    places = [remainder(block + first_tile + k + blocks, blocks) for k in range(tiles + 1)]

    def read(component, row):
        turned = [pltpu.roll(source[place, component, row], cells_y - turn, axis=0) for place in places]
        return [jnp.where(inside, turned[k], turned[k + 1]) for k in range(tiles)]

    return read


class Row:
    def __init__(self, known):
        self.known = dict(known)

    def get(self, *key):
        if key not in self.known:
            getattr(self, "make_" + key[0])(*key[1:-1])
        return self.known[key]

    def all(self, *key):
        return tuple(self.get(*key, item) for item in range(7))

    def put(self, key, values):
        for item, value in enumerate(values):
            self.known[key + (item,)] = value

    def make_cell(self, k):
        raw = [self.get("raw", k, component) for component in range(8)]
        inverse = 1.0 / raw[0]
        self.put(
            ("cell", k),
            (
                raw[0],
                raw[1] * inverse,
                raw[2] * inverse,
                raw[3] * inverse,
                0.5 * (raw[6] + shift(raw[6], -1, 0)),
                0.5 * (raw[7] + shift(raw[7], -1, 1)),
                raw[4] * inverse,
            ),
        )

    def make_centre_x(self, k):
        self.put(("centre_x", k), [0.5 * (self.get("raw", k, 5) + self.get("raw", k + 1, 5))])

    def make_slope(self, k):
        three = [self.all("cell", k + step) for step in (-1, 0, 1)]
        self.put(("slope", k), [0.5 * minmod(h - b, a - h) for b, h, a in zip(*three)])

    def make_along_0(self, face):
        left = [w + s for w, s in zip(self.all("cell", face + 1), self.all("slope", face + 1))]
        right = [w - s for w, s in zip(self.all("cell", face + 2), self.all("slope", face + 2))]
        self.put(("along_0", face), hll_flux(left, right, self.get("raw", face + 2, 5)))

    def sweep(self, k, direction, axis):
        density, vel_x, vel_y, vel_z, centre_y, centre_z, fraction = self.all("cell", k)
        velocity = (vel_x, vel_y, vel_z)
        centres = (self.get("centre_x", k, 0), centre_y, centre_z)
        normal_axis, first_axis, second_axis = sweep_orders[direction]
        states = (
            density,
            velocity[normal_axis],
            velocity[first_axis],
            velocity[second_axis],
            centres[first_axis],
            centres[second_axis],
            fraction,
        )
        left, right = [], []
        for w in states:
            half = 0.5 * minmod(w - shift(w, 1, axis), shift(w, -1, axis) - w)
            left.append(shift(w + half, 1, axis))
            right.append(w - half)
        return hll_flux(left, right, self.get("raw", k, 5 + direction))

    def make_along_1(self, k):
        self.put(("along_1", k), self.sweep(k, 1, 0))

    def make_along_2(self, k):
        self.put(("along_2", k), self.sweep(k, 2, 1))

    def make_out(self):
        along_x = [self.all("along_0", face) for face in range(2)]
        along_y, along_z = self.all("along_1", 2), self.all("along_2", 2)
        edge_z = [
            0.25
            * (
                self.get("along_1", face + 2, 5)
                + self.get("along_1", face + 1, 5)
                - along_x[face][4]
                - shift(along_x[face][4], 1, 0)
            )
            for face in range(2)
        ]
        edge_y = [
            0.25
            * (
                along_x[face][5]
                + shift(along_x[face][5], 1, 1)
                - self.get("along_2", face + 2, 4)
                - self.get("along_2", face + 1, 4)
            )
            for face in range(2)
        ]
        edge_x = 0.25 * (
            along_z[5] + shift(along_z[5], 1, 0) - along_y[4] - shift(along_y[4], 1, 1)
        )
        own = [self.get("raw", 2, component) for component in range(8)]
        places = ((1, 2, 3), (3, 1, 2), (2, 3, 1))
        values = []
        for component in range(5):
            if component == 0:
                slots = (0, 0, 0)
            elif component == 4:
                slots = (6, 6, 6)
            else:
                slots = tuple(places[d][component - 1] for d in range(3))
            through_y, through_z = along_y[slots[1]], along_z[slots[2]]
            total = (
                along_x[1][slots[0]]
                - along_x[0][slots[0]]
                + shift(through_y, -1, 0)
                - through_y
                + shift(through_z, -1, 1)
                - through_z
            )
            values.append(own[component] - time_step * total)
        values.append(
            own[5]
            - time_step * (shift(edge_z[0], -1, 0) - edge_z[0])
            + time_step * (shift(edge_y[0], -1, 1) - edge_y[0])
        )
        values.append(
            own[6]
            - time_step * (shift(edge_x, -1, 1) - edge_x)
            + time_step * (edge_z[1] - edge_z[0])
        )
        values.append(
            own[7]
            - time_step * (edge_y[1] - edge_y[0])
            + time_step * (shift(edge_x, -1, 0) - edge_x)
        )
        self.put(("out",), values)


def message(wanted):
    mains, slots = [], []
    for row, radial in wanted:
        k = radial - row + 2
        if k in (1, 3):
            mains += [(row, "raw", k, component) for component in range(8)]
            slots += [[(row, "raw", k, component)] for component in (0, 1, 2, 5, 6, 7)]
        else:
            mains += [(row, "cell", k, item) for item in range(7)]
            slots += [[(row, "cell", k, item) for item in pair] for pair in ((0, 1), (2, 4), (5,))]
            if k == 4:
                mains.append((row, "raw", k, 5))
                slots.append([(row, "raw", k, 5)])
    return mains, slots


def message_tiles(wanted):
    mains, slots = message(wanted)
    return len(mains) + (len(slots) + 1) // 2


def pack(out, wanted, values):
    mains, slots = message(wanted)
    sub = lax.broadcasted_iota(jnp.int32, out.shape[1:], 0)
    rows = out.shape[1]
    for at, (row, *key) in enumerate(mains):
        out[at] = values[row].get(*key)[:rows]

    def slot(keys):
        around = [values[row].get(*key)[rows:] for row, *key in keys]
        first = around[0]
        tile = jnp.where(sub < 2, first, shift(first, 4, 0))
        if len(around) == 2:
            second = around[1]
            tile = jnp.where(sub == 1, shift(second, 1, 0), tile)
            tile = jnp.where(sub == 2, shift(second, 3, 0), tile)
        return tile

    for at in range(0, len(slots), 2):
        tile = slot(slots[at])
        if at + 1 < len(slots):
            tile = jnp.where(sub < 4, tile, shift(slot(slots[at + 1]), 4, 0))
        out[len(mains) + at // 2] = tile


def unpack(source, wanted, known):
    mains, slots = message(wanted)
    sub = lax.broadcasted_iota(jnp.int32, source.shape[1:], 0)
    edges = {}
    for at, keys in enumerate(slots):
        tile = source[len(mains) + at // 2]
        turned = shift(tile, 4, 0)
        one, two = (tile, turned) if at % 2 == 0 else (turned, tile)
        around = jnp.where(sub < 4, one, two)
        edges[keys[0]] = around
        if len(keys) == 2:
            edges[keys[1]] = jnp.where(sub < 4, shift(around, -1, 0), shift(around, 1, 0))
    for at, key in enumerate(mains):
        main = source[at]
        known[key[0]][key[1:]] = jnp.concatenate([main, edges.get(key, main)], axis=0)


def windows_call(near, far, received, swapped, offset):
    count = len(near)
    parts, cells_x, cells_y, cells_z = near[0].shape
    blocks = 2 * count
    length = blocks * cells_y
    lows, highs = low_windows(cells_x), high_windows(cells_x)

    def body(offset, received, swapped, *refs):
        ins, whole, outs = refs[:blocks], refs[blocks], refs[blocks + 1 :]
        place_x, place_y = lax.axis_index("gx"), lax.axis_index("gy")
        here = remainder(place_x + place_y, 2) == 0
        lane = lax.broadcasted_iota(jnp.int32, (1, cells_x), 1)
        one, other = (
            source[...].reshape(1, cells_x).astype(jnp.float32) for source in (received, swapped)
        )

        def scalars(values):
            return [
                jnp.sum(jnp.where(lane == i, values, 0.0)).astype(jnp.int32) for i in range(cells_x)
            ]

        above, below = scalars(jnp.where(here, one, other)), scalars(jnp.where(here, other, one))
        last = lax.axis_size("gx") - 1
        for side in range(2):
            for step in range(count):
                block = ins[side * count + step]
                place = remainder((place_y ^ side) - 2 * step + blocks, blocks)
                if side == 0 and step == 0:
                    whole[place, : parts // 2] = block[parts // 2 :]
                    whole[place, parts // 2 :] = block[: parts // 2]
                else:
                    whole[place] = block[...]
        sub = lax.broadcasted_iota(jnp.int32, (cells_y, cells_z), 0)
        for out, shift_by, wanted, end, sign, turn in (
            (outs[0], above, lows, last, 1, cells_x),
            (outs[1], below, highs, 0, -1, -cells_x),
        ):
            at_end = place_x == end
            away = jnp.where(at_end, sign * offset[0], 0)
            boost = jnp.where(at_end, sign * shear_speed, 0.0)
            known = {}
            for row, radial in wanted:
                start = remainder(place_y * cells_y - shift_by[row] + away + 2 * length, length)
                read = tile_reader(whole, start, length, -1, 3)
                raw = []
                for component in range(parts):
                    before, main, after = read(component, radial + turn)
                    raw.append(jnp.concatenate([main, jnp.where(sub < 4, after, before)], axis=0))
                raw[2] = raw[2] + boost * raw[0]
                for component in range(parts):
                    known.setdefault(row, {})["raw", radial - row + 2, component] = raw[component]
            pack(out, wanted, {row: Row(found) for row, found in known.items()})

    vmem = pl.BlockSpec(memory_space=pltpu.VMEM)
    smem = pl.BlockSpec(memory_space=pltpu.SMEM)
    return pl.pallas_call(
        body,
        out_shape=[jax.ShapeDtypeStruct((blocks, parts, cells_x, cells_y, cells_z), jnp.float32)]
        + [
            jax.ShapeDtypeStruct((message_tiles(wanted), cells_y, cells_z), jnp.float32)
            for wanted in (lows, highs)
        ],
        in_specs=[smem] + [vmem] * (2 + blocks),
        out_specs=[vmem] * 3,
        compiler_params=pltpu.CompilerParams(vmem_limit_bytes=32 * 1024 * 1024),
        name="windows",
    )(offset, received, swapped, *near, *far)


def reads(key):
    name, *rest = key
    if name == "out":
        found = [("raw", 2, component) for component in range(8)]
        found += [("along_0", face, item) for face in range(2) for item in range(7)]
        found += [(along, 2, item) for along in ("along_1", "along_2") for item in range(7)]
        return found + [(along, k, item) for k in (1, 3) for along, item in (("along_1", 5), ("along_2", 4))]
    if name == "cell":
        return [("raw", rest[0], component) for component in range(8)]
    if name == "centre_x":
        return [("raw", rest[0], 5), ("raw", rest[0] + 1, 5)]
    if name == "slope":
        return [("cell", rest[0] + step, rest[1]) for step in (-1, 0, 1)]
    if name == "along_0":
        cells = [rest[0] + 1, rest[0] + 2]
        found = [(of, k, item) for k in cells for of in ("cell", "slope") for item in range(7)]
        return found + [("raw", cells[1], 5)]
    found = [("cell", rest[0], item) for item in range(7)] + [("centre_x", rest[0], 0)]
    return found + [("raw", rest[0], {"along_1": 6, "along_2": 7}[name])]


def handed_on(cells_x):
    plans = []
    for row in range(cells_x):

        def stage_of_ghost(k):
            return 0 if 0 <= row + k - 2 < cells_x else 1 if row + k - 2 >= cells_x else 2

        stages, readers = {}, {}

        def stage(key):
            if key not in stages:
                given = key[0] == "raw" or (key[0] == "cell" and key[1] in (0, 4) and stage_of_ghost(key[1]))
                if given:
                    stages[key] = stage_of_ghost(key[1])
                else:
                    stages[key] = max(stage(found) for found in reads(key))
                    for found in reads(key):
                        readers.setdefault(found, []).append(key)
            return stages[key]

        ends = [("out", component) for component in range(8)]
        for key in ends:
            stage(key)
        plans.append(
            [
                [
                    key
                    for key, at in stages.items()
                    if at == level
                    and (key in ends or any(stages[reader] > level for reader in readers[key]))
                ]
                for level in range(2)
            ]
        )
    return plans


def own_windows(wholes, row, row_shift, known):
    _, parts, cells_x, cells_y, cells_z = wholes.shape
    length = wholes.shape[0] * cells_y
    sub = lax.broadcasted_iota(jnp.int32, (cells_y, cells_z), 0)
    start = remainder(lax.axis_index("gy") * cells_y - row_shift[row] + length, length)
    read = tile_reader(wholes, start, length, -1, 3)
    for k in range(5):
        radial = row + k - 2
        if 0 <= radial < cells_x:
            for component in range(parts):
                before, main, after = read(component, radial)
                around = jnp.where(sub < 4, after, before)
                known["raw", k, component] = jnp.concatenate([main, around], axis=0)


def inner_call(whole, row_shift):
    _, _, cells_x, cells_y, cells_z = whole.shape
    plans = handed_on(cells_x)

    def body(row_shift, whole, out):
        at = 0
        for row in range(cells_x):
            known = {}
            own_windows(whole, row, row_shift, known)
            values = Row(known)
            for key in plans[row][0]:
                out[at] = values.get(*key)
                at += 1

    vmem = pl.BlockSpec(memory_space=pltpu.VMEM)
    total = sum(len(plan[0]) for plan in plans)
    return pl.pallas_call(
        body,
        out_shape=jax.ShapeDtypeStruct((total, 2 * cells_y, cells_z), jnp.float32),
        in_specs=[pl.BlockSpec(memory_space=pltpu.SMEM), vmem],
        out_specs=vmem,
        compiler_params=pltpu.CompilerParams(vmem_limit_bytes=32 * 1024 * 1024),
        cost_estimate=pl.CostEstimate(flops=10**7, bytes_accessed=10**6, transcendentals=10**5),
        name="inner",
    )(row_shift, whole)


def load_stage(plans, level, ref, known):
    at = 0
    for row, plan in enumerate(plans):
        for key in plan[level]:
            known[row][key] = ref[at]
            at += 1


def middle_call(inner, from_above, cells_x):
    plans = handed_on(cells_x)

    def body(inner, from_above, out):
        known = [{} for _ in range(cells_x)]
        load_stage(plans, 0, inner, known)
        unpack(from_above, high_windows(cells_x), known)
        at = 0
        for row in range(cells_x):
            values = Row(known[row])
            for key in plans[row][1]:
                out[at] = values.get(*key)
                at += 1

    vmem = pl.BlockSpec(memory_space=pltpu.VMEM)
    total = sum(len(plan[1]) for plan in plans)
    return pl.pallas_call(
        body,
        out_shape=jax.ShapeDtypeStruct((total,) + inner.shape[1:], jnp.float32),
        in_specs=[vmem] * 2,
        out_specs=vmem,
        compiler_params=pltpu.CompilerParams(vmem_limit_bytes=32 * 1024 * 1024),
        cost_estimate=pl.CostEstimate(flops=10**6, bytes_accessed=10**6, transcendentals=10**4),
        name="middle",
    )(inner, from_above)


def outer_call(inner, middle, from_below, cells_x, parts):
    cells_y, cells_z = inner.shape[1] // 2, inner.shape[2]
    plans = handed_on(cells_x)

    def body(inner, middle, from_below, out):
        known = [{} for _ in range(cells_x)]
        load_stage(plans, 0, inner, known)
        load_stage(plans, 1, middle, known)
        unpack(from_below, low_windows(cells_x), known)
        for row in range(cells_x):
            values = Row(known[row])
            for component in range(parts):
                out[component, row] = values.get("out", component)[0:cells_y]

    vmem = pl.BlockSpec(memory_space=pltpu.VMEM)
    return pl.pallas_call(
        body,
        out_shape=jax.ShapeDtypeStruct((parts, cells_x, cells_y, cells_z), jnp.float32),
        in_specs=[vmem] * 3,
        out_specs=vmem,
        compiler_params=pltpu.CompilerParams(vmem_limit_bytes=32 * 1024 * 1024),
        name="outer",
    )(inner, middle, from_below)


def on_device(fields, shear_offset, row_shift):
    count_x, count_y = lax.axis_size("gx"), lax.axis_size("gy")
    upward = [(i, (i + 1) % count_x) for i in range(count_x)]
    downward = [(target, source) for source, target in upward]

    def other_core(values):
        return lax.ppermute(values, "gy", [(i, i ^ 1) for i in range(count_y)])

    own = jnp.roll(fields, fields.shape[0] // 2, axis=0)
    meet = []
    for x in range(count_x):
        for y in range(count_y):
            other = (x + 1 if (x + y) % 2 == 0 else x - 1) % count_x
            meet.append((x * count_y + y, other * count_y + y))
    received = lax.ppermute(row_shift, ("gx", "gy"), meet)
    swapped = other_core(received)
    near = [fields] + [
        lax.ppermute(fields, "gy", [(i, (i + step) % count_y) for i in range(count_y)])
        for step in range(2, count_y, 2)
    ]
    passed_on = list(near)
    middle = len(near) // 2
    passed_on[middle], received, swapped = lax.optimization_barrier(
        (near[middle], received, swapped)
    )
    far = [other_core(values) for values in passed_on]
    near[0] = own
    whole, to_above, to_below = windows_call(near, far, received, swapped, shear_offset)
    from_below = lax.ppermute(to_above, "gx", upward)
    from_above = lax.ppermute(to_below, "gx", downward)
    inner = inner_call(whole, row_shift)
    middle = middle_call(inner, from_above, fields.shape[1])
    return outer_call(inner, middle, from_below, fields.shape[1], fields.shape[0])


def solution(mesh):
    placed = (P(None, "gx", "gy", None), P(), P("gx"))
    return jax.shard_map(
        on_device, mesh=mesh, in_specs=placed, out_specs=P(None, "gx", "gy", None), check_vma=False
    )
```

```python
import functools
import jax
import jax.numpy as jnp
from jax import lax
from jax.experimental import pallas as pl
from jax.experimental.pallas import tpu as pltpu
from jax.sharding import PartitionSpec as P

time_step = 0.2
sound_squared = 1.0
shear_speed = 1.5
sweep_orders = ((0, 1, 2), (1, 2, 0), (2, 0, 1))


def remainder(value, by):
    return value & (by - 1) if by & (by - 1) == 0 else lax.rem(value, by)


def quotient(value, by):
    return value >> (by.bit_length() - 1) if by & (by - 1) == 0 else lax.div(value, by)


def minmod(first_diff, second_diff):
    return jnp.maximum(0.0, jnp.minimum(first_diff, second_diff)) + jnp.minimum(
        0.0, jnp.maximum(first_diff, second_diff)
    )


def shift(values, by, axis):
    return pltpu.roll(values, by % values.shape[axis], axis=axis)


def side_terms(state, normal_field):
    density, normal_vel, tang_one, tang_two, field_one, field_two, fraction = state
    normal_square = normal_field * normal_field
    tangent_square = field_one * field_one + field_two * field_two
    mass_flux = density * normal_vel
    dye = density * fraction
    fluxes = (
        mass_flux,
        mass_flux * normal_vel + sound_squared * density + 0.5 * (tangent_square - normal_square),
        mass_flux * tang_one - normal_field * field_one,
        mass_flux * tang_two - normal_field * field_two,
        normal_vel * field_one - tang_one * normal_field,
        normal_vel * field_two - tang_two * normal_field,
        dye * normal_vel,
    )
    conserved = (
        density,
        mass_flux,
        density * tang_one,
        density * tang_two,
        field_one,
        field_two,
        dye,
    )
    inverse = 1.0 / density
    normal_alfven = normal_square * inverse
    tangent_alfven = tangent_square * inverse
    apart = sound_squared - normal_alfven
    spread = (
        apart * apart
        + tangent_alfven * tangent_alfven
        + 2.0 * tangent_alfven * (sound_squared + normal_alfven)
    )
    fast_speed = jnp.sqrt(0.5 * (sound_squared + normal_alfven + tangent_alfven + jnp.sqrt(spread)))
    return (fluxes, conserved, normal_vel - fast_speed, normal_vel + fast_speed)


def hll_flux(left_side, right_side, normal_field):
    flux_left_all, cons_left_all, low_left, high_left = side_terms(left_side, normal_field)
    flux_right_all, cons_right_all, low_right, high_right = side_terms(right_side, normal_field)
    lower_speed = jnp.minimum(jnp.minimum(low_left, low_right), 0.0)
    upper_speed = jnp.maximum(jnp.maximum(high_left, high_right), 0.0)
    inverse_gap = 1.0 / (upper_speed - lower_speed)
    upper = upper_speed * inverse_gap
    lower = lower_speed * inverse_gap
    product = lower_speed * upper
    return tuple(
        upper * flux_left - lower * flux_right + product * (cons_right - cons_left)
        for flux_left, flux_right, cons_left, cons_right in zip(
            flux_left_all, flux_right_all, cons_left_all, cons_right_all
        )
    )


def low_windows(cells_x):
    return [(i, i + k) for i in range(cells_x) for k in (-2, -1) if i + k < 0]


def high_windows(cells_x):
    return [(i, i + k) for i in range(cells_x) for k in (1, 2) if i + k >= cells_x]


def tile_reader(source, start, length, first_tile, tiles):
    cells_y, cells_z = source.shape[3:]
    blocks = length // cells_y
    block = quotient(start, cells_y)
    turn = remainder(start, cells_y)
    inside = lax.broadcasted_iota(jnp.int32, (cells_y, cells_z), 0) < cells_y - turn
    places = [remainder(block + first_tile + k + blocks, blocks) for k in range(tiles + 1)]

    def read(component, row):
        turned = [pltpu.roll(source[place, component, row], cells_y - turn, axis=0) for place in places]
        return [jnp.where(inside, turned[k], turned[k + 1]) for k in range(tiles)]

    return read


class Row:
    def __init__(self, known):
        self.known = dict(known)

    def get(self, *key):
        if key not in self.known:
            getattr(self, "make_" + key[0])(*key[1:-1])
        return self.known[key]

    def all(self, *key):
        return tuple(self.get(*key, item) for item in range(7))

    def put(self, key, values):
        for item, value in enumerate(values):
            self.known[key + (item,)] = value

    def make_cell(self, k):
        raw = [self.get("raw", k, component) for component in range(8)]
        inverse = 1.0 / raw[0]
        self.put(
            ("cell", k),
            (
                raw[0],
                raw[1] * inverse,
                raw[2] * inverse,
                raw[3] * inverse,
                0.5 * (raw[6] + shift(raw[6], -1, 0)),
                0.5 * (raw[7] + shift(raw[7], -1, 1)),
                raw[4] * inverse,
            ),
        )

    def make_centre_x(self, k):
        self.put(("centre_x", k), [0.5 * (self.get("raw", k, 5) + self.get("raw", k + 1, 5))])

    def make_slope(self, k):
        three = [self.all("cell", k + step) for step in (-1, 0, 1)]
        self.put(("slope", k), [0.5 * minmod(h - b, a - h) for b, h, a in zip(*three)])

    def make_along_0(self, face):
        left = [w + s for w, s in zip(self.all("cell", face + 1), self.all("slope", face + 1))]
        right = [w - s for w, s in zip(self.all("cell", face + 2), self.all("slope", face + 2))]
        self.put(("along_0", face), hll_flux(left, right, self.get("raw", face + 2, 5)))

    def sweep(self, k, direction, axis):
        density, vel_x, vel_y, vel_z, centre_y, centre_z, fraction = self.all("cell", k)
        velocity = (vel_x, vel_y, vel_z)
        centres = (self.get("centre_x", k, 0), centre_y, centre_z)
        normal_axis, first_axis, second_axis = sweep_orders[direction]
        states = (
            density,
            velocity[normal_axis],
            velocity[first_axis],
            velocity[second_axis],
            centres[first_axis],
            centres[second_axis],
            fraction,
        )
        left, right = [], []
        for w in states:
            half = 0.5 * minmod(w - shift(w, 1, axis), shift(w, -1, axis) - w)
            left.append(shift(w + half, 1, axis))
            right.append(w - half)
        return hll_flux(left, right, self.get("raw", k, 5 + direction))

    def make_along_1(self, k):
        self.put(("along_1", k), self.sweep(k, 1, 0))

    def make_along_2(self, k):
        self.put(("along_2", k), self.sweep(k, 2, 1))

    def make_out(self):
        along_x = [self.all("along_0", face) for face in range(2)]
        along_y, along_z = self.all("along_1", 2), self.all("along_2", 2)
        edge_z = [
            0.25
            * (
                self.get("along_1", face + 2, 5)
                + self.get("along_1", face + 1, 5)
                - along_x[face][4]
                - shift(along_x[face][4], 1, 0)
            )
            for face in range(2)
        ]
        edge_y = [
            0.25
            * (
                along_x[face][5]
                + shift(along_x[face][5], 1, 1)
                - self.get("along_2", face + 2, 4)
                - self.get("along_2", face + 1, 4)
            )
            for face in range(2)
        ]
        edge_x = 0.25 * (
            along_z[5] + shift(along_z[5], 1, 0) - along_y[4] - shift(along_y[4], 1, 1)
        )
        own = [self.get("raw", 2, component) for component in range(8)]
        places = ((1, 2, 3), (3, 1, 2), (2, 3, 1))
        values = []
        for component in range(5):
            if component == 0:
                slots = (0, 0, 0)
            elif component == 4:
                slots = (6, 6, 6)
            else:
                slots = tuple(places[d][component - 1] for d in range(3))
            through_y, through_z = along_y[slots[1]], along_z[slots[2]]
            total = (
                along_x[1][slots[0]]
                - along_x[0][slots[0]]
                + shift(through_y, -1, 0)
                - through_y
                + shift(through_z, -1, 1)
                - through_z
            )
            values.append(own[component] - time_step * total)
        values.append(
            own[5]
            - time_step * (shift(edge_z[0], -1, 0) - edge_z[0])
            + time_step * (shift(edge_y[0], -1, 1) - edge_y[0])
        )
        values.append(
            own[6]
            - time_step * (shift(edge_x, -1, 1) - edge_x)
            + time_step * (edge_z[1] - edge_z[0])
        )
        values.append(
            own[7]
            - time_step * (edge_y[1] - edge_y[0])
            + time_step * (shift(edge_x, -1, 0) - edge_x)
        )
        self.put(("out",), values)


def message(wanted):
    mains, slots = [], []
    for row, radial in wanted:
        k = radial - row + 2
        if k in (1, 3):
            mains += [(row, "raw", k, component) for component in range(8)]
            slots += [[(row, "raw", k, component)] for component in (0, 1, 2, 5, 6, 7)]
        else:
            mains += [(row, "cell", k, item) for item in range(7)]
            slots += [[(row, "cell", k, item) for item in pair] for pair in ((0, 1), (2, 4), (5,))]
            if k == 4:
                mains.append((row, "raw", k, 5))
                slots.append([(row, "raw", k, 5)])
    return mains, slots


def message_tiles(wanted):
    mains, slots = message(wanted)
    return len(mains) + (len(slots) + 1) // 2


def pack(out, wanted, values):
    mains, slots = message(wanted)
    sub = lax.broadcasted_iota(jnp.int32, out.shape[1:], 0)
    rows = out.shape[1]
    for at, (row, *key) in enumerate(mains):
        out[at] = values[row].get(*key)[:rows]

    def slot(keys):
        around = [values[row].get(*key)[rows:] for row, *key in keys]
        first = around[0]
        tile = jnp.where(sub < 2, first, shift(first, 4, 0))
        if len(around) == 2:
            second = around[1]
            tile = jnp.where(sub == 1, shift(second, 1, 0), tile)
            tile = jnp.where(sub == 2, shift(second, 3, 0), tile)
        return tile

    for at in range(0, len(slots), 2):
        tile = slot(slots[at])
        if at + 1 < len(slots):
            tile = jnp.where(sub < 4, tile, shift(slot(slots[at + 1]), 4, 0))
        out[len(mains) + at // 2] = tile


def unpack(source, wanted, known):
    mains, slots = message(wanted)
    sub = lax.broadcasted_iota(jnp.int32, source.shape[1:], 0)
    edges = {}
    for at, keys in enumerate(slots):
        tile = source[len(mains) + at // 2]
        turned = shift(tile, 4, 0)
        one, two = (tile, turned) if at % 2 == 0 else (turned, tile)
        around = jnp.where(sub < 4, one, two)
        edges[keys[0]] = around
        if len(keys) == 2:
            edges[keys[1]] = jnp.where(sub < 4, shift(around, -1, 0), shift(around, 1, 0))
    for at, key in enumerate(mains):
        main = source[at]
        known[key[0]][key[1:]] = jnp.concatenate([main, edges.get(key, main)], axis=0)


def windows_call(near, far, received, swapped, offset):
    count = len(near)
    parts, cells_x, cells_y, cells_z = near[0].shape
    blocks = 2 * count
    length = blocks * cells_y
    lows, highs = low_windows(cells_x), high_windows(cells_x)

    def body(offset, received, swapped, *refs):
        ins, whole, outs = refs[:blocks], refs[blocks], refs[blocks + 1 :]
        place_x, place_y = lax.axis_index("gx"), lax.axis_index("gy")
        here = remainder(place_x + place_y, 2) == 0
        lane = lax.broadcasted_iota(jnp.int32, (1, cells_x), 1)
        one, other = (
            source[...].reshape(1, cells_x).astype(jnp.float32) for source in (received, swapped)
        )

        def scalars(values):
            return [
                jnp.sum(jnp.where(lane == i, values, 0.0)).astype(jnp.int32) for i in range(cells_x)
            ]

        above, below = scalars(jnp.where(here, one, other)), scalars(jnp.where(here, other, one))
        last = lax.axis_size("gx") - 1
        for side in range(2):
            for step in range(count):
                block = ins[side * count + step]
                place = remainder((place_y ^ side) - 2 * step + blocks, blocks)
                if side == 0 and step == 0:
                    whole[place, : parts // 2] = block[parts // 2 :]
                    whole[place, parts // 2 :] = block[: parts // 2]
                else:
                    whole[place] = block[...]
        sub = lax.broadcasted_iota(jnp.int32, (cells_y, cells_z), 0)
        for out, shift_by, wanted, end, sign, turn in (
            (outs[0], above, lows, last, 1, cells_x),
            (outs[1], below, highs, 0, -1, -cells_x),
        ):
            at_end = place_x == end
            away = jnp.where(at_end, sign * offset[0], 0)
            boost = jnp.where(at_end, sign * shear_speed, 0.0)
            known = {}
            for row, radial in wanted:
                start = remainder(place_y * cells_y - shift_by[row] + away + 2 * length, length)
                read = tile_reader(whole, start, length, -1, 3)
                raw = []
                for component in range(parts):
                    before, main, after = read(component, radial + turn)
                    raw.append(jnp.concatenate([main, jnp.where(sub < 4, after, before)], axis=0))
                raw[2] = raw[2] + boost * raw[0]
                for component in range(parts):
                    known.setdefault(row, {})["raw", radial - row + 2, component] = raw[component]
            pack(out, wanted, {row: Row(found) for row, found in known.items()})

    vmem = pl.BlockSpec(memory_space=pltpu.VMEM)
    smem = pl.BlockSpec(memory_space=pltpu.SMEM)
    return pl.pallas_call(
        body,
        out_shape=[jax.ShapeDtypeStruct((blocks, parts, cells_x, cells_y, cells_z), jnp.float32)]
        + [
            jax.ShapeDtypeStruct((message_tiles(wanted), cells_y, cells_z), jnp.float32)
            for wanted in (lows, highs)
        ],
        in_specs=[smem] + [vmem] * (2 + blocks),
        out_specs=[vmem] * 3,
        compiler_params=pltpu.CompilerParams(vmem_limit_bytes=32 * 1024 * 1024),
        name="windows",
    )(offset, received, swapped, *near, *far)


def reads(key):
    name, *rest = key
    if name == "out":
        found = [("raw", 2, component) for component in range(8)]
        found += [("along_0", face, item) for face in range(2) for item in range(7)]
        found += [(along, 2, item) for along in ("along_1", "along_2") for item in range(7)]
        return found + [(along, k, item) for k in (1, 3) for along, item in (("along_1", 5), ("along_2", 4))]
    if name == "cell":
        return [("raw", rest[0], component) for component in range(8)]
    if name == "centre_x":
        return [("raw", rest[0], 5), ("raw", rest[0] + 1, 5)]
    if name == "slope":
        return [("cell", rest[0] + step, rest[1]) for step in (-1, 0, 1)]
    if name == "along_0":
        cells = [rest[0] + 1, rest[0] + 2]
        found = [(of, k, item) for k in cells for of in ("cell", "slope") for item in range(7)]
        return found + [("raw", cells[1], 5)]
    found = [("cell", rest[0], item) for item in range(7)] + [("centre_x", rest[0], 0)]
    return found + [("raw", rest[0], {"along_1": 6, "along_2": 7}[name])]


def handed_on(cells_x):
    plans = []
    for row in range(cells_x):

        def stage_of_ghost(k):
            return 0 if 0 <= row + k - 2 < cells_x else 1 if row + k - 2 >= cells_x else 2

        stages, readers = {}, {}

        def stage(key):
            if key not in stages:
                given = key[0] == "raw" or (key[0] == "cell" and key[1] in (0, 4) and stage_of_ghost(key[1]))
                if given:
                    stages[key] = stage_of_ghost(key[1])
                else:
                    stages[key] = max(stage(found) for found in reads(key))
                    for found in reads(key):
                        readers.setdefault(found, []).append(key)
            return stages[key]

        ends = [("out", component) for component in range(8)]
        for key in ends:
            stage(key)
        plans.append(
            [
                [
                    key
                    for key, at in stages.items()
                    if at == level
                    and (key in ends or any(stages[reader] > level for reader in readers[key]))
                ]
                for level in range(2)
            ]
        )
    return plans


def own_windows(wholes, row, row_shift, known):
    _, parts, cells_x, cells_y, cells_z = wholes.shape
    length = wholes.shape[0] * cells_y
    sub = lax.broadcasted_iota(jnp.int32, (cells_y, cells_z), 0)
    start = remainder(lax.axis_index("gy") * cells_y - row_shift[row] + length, length)
    read = tile_reader(wholes, start, length, -1, 3)
    for k in range(5):
        radial = row + k - 2
        if 0 <= radial < cells_x:
            for component in range(parts):
                before, main, after = read(component, radial)
                around = jnp.where(sub < 4, after, before)
                known["raw", k, component] = jnp.concatenate([main, around], axis=0)


def inner_call(whole, row_shift):
    _, _, cells_x, cells_y, cells_z = whole.shape
    plans = handed_on(cells_x)

    def body(row_shift, whole, out):
        at = 0
        for row in range(cells_x):
            known = {}
            own_windows(whole, row, row_shift, known)
            values = Row(known)
            for key in plans[row][0]:
                out[at] = values.get(*key)
                at += 1

    vmem = pl.BlockSpec(memory_space=pltpu.VMEM)
    total = sum(len(plan[0]) for plan in plans)
    return pl.pallas_call(
        body,
        out_shape=jax.ShapeDtypeStruct((total, 2 * cells_y, cells_z), jnp.float32),
        in_specs=[pl.BlockSpec(memory_space=pltpu.SMEM), vmem],
        out_specs=vmem,
        compiler_params=pltpu.CompilerParams(vmem_limit_bytes=32 * 1024 * 1024),
        cost_estimate=pl.CostEstimate(flops=10**7, bytes_accessed=10**6, transcendentals=10**5),
        name="inner",
    )(row_shift, whole)


def load_stage(plans, level, ref, known):
    at = 0
    for row, plan in enumerate(plans):
        for key in plan[level]:
            known[row][key] = ref[at]
            at += 1


def middle_call(inner, from_above, cells_x):
    plans = handed_on(cells_x)

    def body(inner, from_above, out):
        known = [{} for _ in range(cells_x)]
        load_stage(plans, 0, inner, known)
        unpack(from_above, high_windows(cells_x), known)
        at = 0
        for row in range(cells_x):
            values = Row(known[row])
            for key in plans[row][1]:
                out[at] = values.get(*key)
                at += 1

    vmem = pl.BlockSpec(memory_space=pltpu.VMEM)
    total = sum(len(plan[1]) for plan in plans)
    return pl.pallas_call(
        body,
        out_shape=jax.ShapeDtypeStruct((total,) + inner.shape[1:], jnp.float32),
        in_specs=[vmem] * 2,
        out_specs=vmem,
        compiler_params=pltpu.CompilerParams(vmem_limit_bytes=32 * 1024 * 1024),
        cost_estimate=pl.CostEstimate(flops=10**6, bytes_accessed=10**6, transcendentals=10**4),
        name="middle",
    )(inner, from_above)


def outer_call(inner, middle, from_below, cells_x, parts):
    cells_y, cells_z = inner.shape[1] // 2, inner.shape[2]
    plans = handed_on(cells_x)

    def body(inner, middle, from_below, out):
        known = [{} for _ in range(cells_x)]
        load_stage(plans, 0, inner, known)
        load_stage(plans, 1, middle, known)
        unpack(from_below, low_windows(cells_x), known)
        for row in range(cells_x):
            values = Row(known[row])
            for component in range(parts):
                out[component, row] = values.get("out", component)[0:cells_y]

    vmem = pl.BlockSpec(memory_space=pltpu.VMEM)
    return pl.pallas_call(
        body,
        out_shape=jax.ShapeDtypeStruct((parts, cells_x, cells_y, cells_z), jnp.float32),
        in_specs=[vmem] * 3,
        out_specs=vmem,
        compiler_params=pltpu.CompilerParams(vmem_limit_bytes=32 * 1024 * 1024),
        name="outer",
    )(inner, middle, from_below)


def on_device(fields, shear_offset, row_shift):
    count_x, count_y = lax.axis_size("gx"), lax.axis_size("gy")
    upward = [(i, (i + 1) % count_x) for i in range(count_x)]
    downward = [(target, source) for source, target in upward]

    def other_core(values):
        return lax.ppermute(values, "gy", [(i, i ^ 1) for i in range(count_y)])

    own = jnp.roll(fields, fields.shape[0] // 2, axis=0)
    meet = []
    for x in range(count_x):
        for y in range(count_y):
            other = (x + 1 if (x + y) % 2 == 0 else x - 1) % count_x
            meet.append((x * count_y + y, other * count_y + y))
    received = lax.ppermute(row_shift, ("gx", "gy"), meet)
    received, own = lax.optimization_barrier((received, own))
    swapped = other_core(received)
    near = [fields] + [
        lax.ppermute(fields, "gy", [(i, (i + step) % count_y) for i in range(count_y)])
        for step in range(2, count_y, 2)
    ]
    passed_on = list(near)
    far = [other_core(near[0]), other_core(near[1])]
    passed_on[2], received, swapped, _ = lax.optimization_barrier((near[2], received, swapped, far[1]))
    far.append(other_core(passed_on[2]))
    passed_on[3], _ = lax.optimization_barrier((near[3], passed_on[2]))
    far += [other_core(values) for values in passed_on[3:]]
    near[0] = own
    whole, to_above, to_below = windows_call(near, far, received, swapped, shear_offset)
    from_below = lax.ppermute(to_above, "gx", upward)
    from_above = lax.ppermute(to_below, "gx", downward)
    inner = inner_call(whole, row_shift)
    middle = middle_call(inner, from_above, fields.shape[1])
    return outer_call(inner, middle, from_below, fields.shape[1], fields.shape[0])


def solution(mesh):
    placed = (P(None, "gx", "gy", None), P(), P("gx"))
    return jax.shard_map(
        on_device, mesh=mesh, in_specs=placed, out_specs=P(None, "gx", "gy", None), check_vma=False
    )
```

```python
import functools
import jax
import jax.numpy as jnp
from jax import lax
from jax.experimental import pallas as pl
from jax.experimental.pallas import tpu as pltpu
from jax.sharding import PartitionSpec as P

time_step = 0.2
sound_squared = 1.0
shear_speed = 1.5
sweep_orders = ((0, 1, 2), (1, 2, 0), (2, 0, 1))


def remainder(value, by):
    return value & (by - 1) if by & (by - 1) == 0 else lax.rem(value, by)


def quotient(value, by):
    return value >> (by.bit_length() - 1) if by & (by - 1) == 0 else lax.div(value, by)


def minmod(first_diff, second_diff):
    return jnp.maximum(0.0, jnp.minimum(first_diff, second_diff)) + jnp.minimum(
        0.0, jnp.maximum(first_diff, second_diff)
    )


def shift(values, by, axis):
    return pltpu.roll(values, by % values.shape[axis], axis=axis)


def side_terms(state, normal_field):
    density, normal_vel, tang_one, tang_two, field_one, field_two, fraction = state
    normal_square = normal_field * normal_field
    tangent_square = field_one * field_one + field_two * field_two
    mass_flux = density * normal_vel
    dye = density * fraction
    fluxes = (
        mass_flux,
        mass_flux * normal_vel + sound_squared * density + 0.5 * (tangent_square - normal_square),
        mass_flux * tang_one - normal_field * field_one,
        mass_flux * tang_two - normal_field * field_two,
        normal_vel * field_one - tang_one * normal_field,
        normal_vel * field_two - tang_two * normal_field,
        dye * normal_vel,
    )
    conserved = (
        density,
        mass_flux,
        density * tang_one,
        density * tang_two,
        field_one,
        field_two,
        dye,
    )
    inverse = 1.0 / density
    normal_alfven = normal_square * inverse
    tangent_alfven = tangent_square * inverse
    apart = sound_squared - normal_alfven
    spread = (
        apart * apart
        + tangent_alfven * tangent_alfven
        + 2.0 * tangent_alfven * (sound_squared + normal_alfven)
    )
    fast_speed = jnp.sqrt(0.5 * (sound_squared + normal_alfven + tangent_alfven + jnp.sqrt(spread)))
    return (fluxes, conserved, normal_vel - fast_speed, normal_vel + fast_speed)


def hll_flux(left_side, right_side, normal_field):
    flux_left_all, cons_left_all, low_left, high_left = side_terms(left_side, normal_field)
    flux_right_all, cons_right_all, low_right, high_right = side_terms(right_side, normal_field)
    lower_speed = jnp.minimum(jnp.minimum(low_left, low_right), 0.0)
    upper_speed = jnp.maximum(jnp.maximum(high_left, high_right), 0.0)
    inverse_gap = 1.0 / (upper_speed - lower_speed)
    upper = upper_speed * inverse_gap
    lower = lower_speed * inverse_gap
    product = lower_speed * upper
    return tuple(
        upper * flux_left - lower * flux_right + product * (cons_right - cons_left)
        for flux_left, flux_right, cons_left, cons_right in zip(
            flux_left_all, flux_right_all, cons_left_all, cons_right_all
        )
    )


def low_windows(cells_x):
    return [(i, i + k) for i in range(cells_x) for k in (-2, -1) if i + k < 0]


def high_windows(cells_x):
    return [(i, i + k) for i in range(cells_x) for k in (1, 2) if i + k >= cells_x]


def tile_reader(source, start, length, first_tile, tiles):
    cells_y, cells_z = source.shape[3:]
    blocks = length // cells_y
    block = quotient(start, cells_y)
    turn = remainder(start, cells_y)
    inside = lax.broadcasted_iota(jnp.int32, (cells_y, cells_z), 0) < cells_y - turn
    places = [remainder(block + first_tile + k + blocks, blocks) for k in range(tiles + 1)]

    def read(component, row):
        turned = [pltpu.roll(source[place, component, row], cells_y - turn, axis=0) for place in places]
        return [jnp.where(inside, turned[k], turned[k + 1]) for k in range(tiles)]

    return read


class Row:
    def __init__(self, known):
        self.known = dict(known)

    def get(self, *key):
        if key not in self.known:
            getattr(self, "make_" + key[0])(*key[1:-1])
        return self.known[key]

    def all(self, *key):
        return tuple(self.get(*key, item) for item in range(7))

    def put(self, key, values):
        for item, value in enumerate(values):
            self.known[key + (item,)] = value

    def make_cell(self, k):
        raw = [self.get("raw", k, component) for component in range(8)]
        inverse = 1.0 / raw[0]
        self.put(
            ("cell", k),
            (
                raw[0],
                raw[1] * inverse,
                raw[2] * inverse,
                raw[3] * inverse,
                0.5 * (raw[6] + shift(raw[6], -1, 0)),
                0.5 * (raw[7] + shift(raw[7], -1, 1)),
                raw[4] * inverse,
            ),
        )

    def make_centre_x(self, k):
        self.put(("centre_x", k), [0.5 * (self.get("raw", k, 5) + self.get("raw", k + 1, 5))])

    def make_slope(self, k):
        three = [self.all("cell", k + step) for step in (-1, 0, 1)]
        self.put(("slope", k), [0.5 * minmod(h - b, a - h) for b, h, a in zip(*three)])

    def make_along_0(self, face):
        left = [w + s for w, s in zip(self.all("cell", face + 1), self.all("slope", face + 1))]
        right = [w - s for w, s in zip(self.all("cell", face + 2), self.all("slope", face + 2))]
        self.put(("along_0", face), hll_flux(left, right, self.get("raw", face + 2, 5)))

    def sweep(self, k, direction, axis):
        density, vel_x, vel_y, vel_z, centre_y, centre_z, fraction = self.all("cell", k)
        velocity = (vel_x, vel_y, vel_z)
        centres = (self.get("centre_x", k, 0), centre_y, centre_z)
        normal_axis, first_axis, second_axis = sweep_orders[direction]
        states = (
            density,
            velocity[normal_axis],
            velocity[first_axis],
            velocity[second_axis],
            centres[first_axis],
            centres[second_axis],
            fraction,
        )
        left, right = [], []
        for w in states:
            half = 0.5 * minmod(w - shift(w, 1, axis), shift(w, -1, axis) - w)
            left.append(shift(w + half, 1, axis))
            right.append(w - half)
        return hll_flux(left, right, self.get("raw", k, 5 + direction))

    def make_along_1(self, k):
        self.put(("along_1", k), self.sweep(k, 1, 0))

    def make_along_2(self, k):
        self.put(("along_2", k), self.sweep(k, 2, 1))

    def make_out(self):
        along_x = [self.all("along_0", face) for face in range(2)]
        along_y, along_z = self.all("along_1", 2), self.all("along_2", 2)
        edge_z = [
            0.25
            * (
                self.get("along_1", face + 2, 5)
                + self.get("along_1", face + 1, 5)
                - along_x[face][4]
                - shift(along_x[face][4], 1, 0)
            )
            for face in range(2)
        ]
        edge_y = [
            0.25
            * (
                along_x[face][5]
                + shift(along_x[face][5], 1, 1)
                - self.get("along_2", face + 2, 4)
                - self.get("along_2", face + 1, 4)
            )
            for face in range(2)
        ]
        edge_x = 0.25 * (
            along_z[5] + shift(along_z[5], 1, 0) - along_y[4] - shift(along_y[4], 1, 1)
        )
        own = [self.get("raw", 2, component) for component in range(8)]
        places = ((1, 2, 3), (3, 1, 2), (2, 3, 1))
        values = []
        for component in range(5):
            if component == 0:
                slots = (0, 0, 0)
            elif component == 4:
                slots = (6, 6, 6)
            else:
                slots = tuple(places[d][component - 1] for d in range(3))
            through_y, through_z = along_y[slots[1]], along_z[slots[2]]
            total = (
                along_x[1][slots[0]]
                - along_x[0][slots[0]]
                + shift(through_y, -1, 0)
                - through_y
                + shift(through_z, -1, 1)
                - through_z
            )
            values.append(own[component] - time_step * total)
        values.append(
            own[5]
            - time_step * (shift(edge_z[0], -1, 0) - edge_z[0])
            + time_step * (shift(edge_y[0], -1, 1) - edge_y[0])
        )
        values.append(
            own[6]
            - time_step * (shift(edge_x, -1, 1) - edge_x)
            + time_step * (edge_z[1] - edge_z[0])
        )
        values.append(
            own[7]
            - time_step * (edge_y[1] - edge_y[0])
            + time_step * (shift(edge_x, -1, 0) - edge_x)
        )
        self.put(("out",), values)


def message(wanted):
    mains, slots = [], []
    for row, radial in wanted:
        k = radial - row + 2
        if k in (1, 3):
            mains += [(row, "raw", k, component) for component in range(8)]
            slots += [[(row, "raw", k, component)] for component in (0, 1, 2, 5, 6, 7)]
        else:
            mains += [(row, "cell", k, item) for item in range(7)]
            slots += [[(row, "cell", k, item) for item in pair] for pair in ((0, 1), (2, 4), (5,))]
            if k == 4:
                mains.append((row, "raw", k, 5))
                slots.append([(row, "raw", k, 5)])
    return mains, slots


def message_tiles(wanted):
    mains, slots = message(wanted)
    return len(mains) + (len(slots) + 1) // 2


def pack(out, wanted, values):
    mains, slots = message(wanted)
    sub = lax.broadcasted_iota(jnp.int32, out.shape[1:], 0)
    rows = out.shape[1]
    for at, (row, *key) in enumerate(mains):
        out[at] = values[row].get(*key)[:rows]

    def slot(keys):
        around = [values[row].get(*key)[rows:] for row, *key in keys]
        first = around[0]
        tile = jnp.where(sub < 2, first, shift(first, 4, 0))
        if len(around) == 2:
            second = around[1]
            tile = jnp.where(sub == 1, shift(second, 1, 0), tile)
            tile = jnp.where(sub == 2, shift(second, 3, 0), tile)
        return tile

    for at in range(0, len(slots), 2):
        tile = slot(slots[at])
        if at + 1 < len(slots):
            tile = jnp.where(sub < 4, tile, shift(slot(slots[at + 1]), 4, 0))
        out[len(mains) + at // 2] = tile


def unpack(source, wanted, known):
    mains, slots = message(wanted)
    sub = lax.broadcasted_iota(jnp.int32, source.shape[1:], 0)
    edges = {}
    for at, keys in enumerate(slots):
        tile = source[len(mains) + at // 2]
        turned = shift(tile, 4, 0)
        one, two = (tile, turned) if at % 2 == 0 else (turned, tile)
        around = jnp.where(sub < 4, one, two)
        edges[keys[0]] = around
        if len(keys) == 2:
            edges[keys[1]] = jnp.where(sub < 4, shift(around, -1, 0), shift(around, 1, 0))
    for at, key in enumerate(mains):
        main = source[at]
        known[key[0]][key[1:]] = jnp.concatenate([main, edges.get(key, main)], axis=0)


def windows_down_call(near, far, received, swapped, offset):
    count = len(near)
    parts, cells_x, cells_y, cells_z = near[0].shape
    blocks = 2 * count
    length = blocks * cells_y
    lows, highs = low_windows(cells_x), high_windows(cells_x)

    def body(offset, received, swapped, *refs):
        ins, whole, outs = refs[:blocks], refs[blocks], refs[blocks + 1 :]
        place_x, place_y = lax.axis_index("gx"), lax.axis_index("gy")
        here = remainder(place_x + place_y, 2) == 0
        lane = lax.broadcasted_iota(jnp.int32, (1, cells_x), 1)
        one, other = (
            source[...].reshape(1, cells_x).astype(jnp.float32) for source in (received, swapped)
        )

        def scalars(values):
            return [
                jnp.sum(jnp.where(lane == i, values, 0.0)).astype(jnp.int32) for i in range(cells_x)
            ]

        above, below = scalars(jnp.where(here, one, other)), scalars(jnp.where(here, other, one))
        last = lax.axis_size("gx") - 1
        for side in range(2):
            for step in range(count):
                block = ins[side * count + step]
                place = remainder((place_y ^ side) - 2 * step + blocks, blocks)
                if side == 0 and step == 0:
                    whole[place, : parts // 2] = block[parts // 2 :]
                    whole[place, parts // 2 :] = block[: parts // 2]
                else:
                    whole[place] = block[...]
        sub = lax.broadcasted_iota(jnp.int32, (cells_y, cells_z), 0)
        for out, shift_by, wanted, end, sign, turn in (
            (outs[0], below, highs, 0, -1, -cells_x),
        ):
            at_end = place_x == end
            away = jnp.where(at_end, sign * offset[0], 0)
            boost = jnp.where(at_end, sign * shear_speed, 0.0)
            known = {}
            for row, radial in wanted:
                start = remainder(place_y * cells_y - shift_by[row] + away + 2 * length, length)
                read = tile_reader(whole, start, length, -1, 3)
                raw = []
                for component in range(parts):
                    before, main, after = read(component, radial + turn)
                    raw.append(jnp.concatenate([main, jnp.where(sub < 4, after, before)], axis=0))
                raw[2] = raw[2] + boost * raw[0]
                for component in range(parts):
                    known.setdefault(row, {})["raw", radial - row + 2, component] = raw[component]
            pack(out, wanted, {row: Row(found) for row, found in known.items()})

    vmem = pl.BlockSpec(memory_space=pltpu.VMEM)
    smem = pl.BlockSpec(memory_space=pltpu.SMEM)
    return pl.pallas_call(
        body,
        out_shape=[jax.ShapeDtypeStruct((blocks, parts, cells_x, cells_y, cells_z), jnp.float32)]
        + [
            jax.ShapeDtypeStruct((message_tiles(wanted), cells_y, cells_z), jnp.float32)
            for wanted in (highs,)
        ],
        in_specs=[smem] + [vmem] * (2 + blocks),
        out_specs=[vmem] * 2,
        cost_estimate=pl.CostEstimate(flops=1, bytes_accessed=1, transcendentals=0),
        compiler_params=pltpu.CompilerParams(vmem_limit_bytes=32 * 1024 * 1024),
        name="windows_down",
    )(offset, received, swapped, *near, *far)


def windows_up_call(whole, received, swapped, offset):
    blocks, parts, cells_x, cells_y, cells_z = whole.shape
    length = blocks * cells_y
    lows, highs = low_windows(cells_x), high_windows(cells_x)

    def body(offset, received, swapped, whole, *outs):
        place_x, place_y = lax.axis_index("gx"), lax.axis_index("gy")
        here = remainder(place_x + place_y, 2) == 0
        lane = lax.broadcasted_iota(jnp.int32, (1, cells_x), 1)
        one, other = (
            source[...].reshape(1, cells_x).astype(jnp.float32) for source in (received, swapped)
        )

        def scalars(values):
            return [
                jnp.sum(jnp.where(lane == i, values, 0.0)).astype(jnp.int32) for i in range(cells_x)
            ]

        above, below = scalars(jnp.where(here, one, other)), scalars(jnp.where(here, other, one))
        last = lax.axis_size("gx") - 1
        sub = lax.broadcasted_iota(jnp.int32, (cells_y, cells_z), 0)
        for out, shift_by, wanted, end, sign, turn in (
            (outs[0], above, lows, last, 1, cells_x),
        ):
            at_end = place_x == end
            away = jnp.where(at_end, sign * offset[0], 0)
            boost = jnp.where(at_end, sign * shear_speed, 0.0)
            known = {}
            for row, radial in wanted:
                start = remainder(place_y * cells_y - shift_by[row] + away + 2 * length, length)
                read = tile_reader(whole, start, length, -1, 3)
                raw = []
                for component in range(parts):
                    before, main, after = read(component, radial + turn)
                    raw.append(jnp.concatenate([main, jnp.where(sub < 4, after, before)], axis=0))
                raw[2] = raw[2] + boost * raw[0]
                for component in range(parts):
                    known.setdefault(row, {})["raw", radial - row + 2, component] = raw[component]
            pack(out, wanted, {row: Row(found) for row, found in known.items()})

    vmem = pl.BlockSpec(memory_space=pltpu.VMEM)
    smem = pl.BlockSpec(memory_space=pltpu.SMEM)
    return pl.pallas_call(
        body,
        out_shape=jax.ShapeDtypeStruct((message_tiles(lows), cells_y, cells_z), jnp.float32),
        in_specs=[smem] + [vmem] * 3,
        out_specs=vmem,
        cost_estimate=pl.CostEstimate(flops=1, bytes_accessed=1, transcendentals=0),
        compiler_params=pltpu.CompilerParams(vmem_limit_bytes=32 * 1024 * 1024),
        name="windows_up",
    )(offset, received, swapped, whole)


def reads(key):
    name, *rest = key
    if name == "out":
        found = [("raw", 2, component) for component in range(8)]
        found += [("along_0", face, item) for face in range(2) for item in range(7)]
        found += [(along, 2, item) for along in ("along_1", "along_2") for item in range(7)]
        return found + [(along, k, item) for k in (1, 3) for along, item in (("along_1", 5), ("along_2", 4))]
    if name == "cell":
        return [("raw", rest[0], component) for component in range(8)]
    if name == "centre_x":
        return [("raw", rest[0], 5), ("raw", rest[0] + 1, 5)]
    if name == "slope":
        return [("cell", rest[0] + step, rest[1]) for step in (-1, 0, 1)]
    if name == "along_0":
        cells = [rest[0] + 1, rest[0] + 2]
        found = [(of, k, item) for k in cells for of in ("cell", "slope") for item in range(7)]
        return found + [("raw", cells[1], 5)]
    found = [("cell", rest[0], item) for item in range(7)] + [("centre_x", rest[0], 0)]
    return found + [("raw", rest[0], {"along_1": 6, "along_2": 7}[name])]


def handed_on(cells_x):
    plans = []
    for row in range(cells_x):

        def stage_of_ghost(k):
            return 0 if 0 <= row + k - 2 < cells_x else 1 if row + k - 2 >= cells_x else 2

        stages, readers = {}, {}

        def stage(key):
            if key not in stages:
                given = key[0] == "raw" or (key[0] == "cell" and key[1] in (0, 4) and stage_of_ghost(key[1]))
                if given:
                    stages[key] = stage_of_ghost(key[1])
                else:
                    stages[key] = max(stage(found) for found in reads(key))
                    for found in reads(key):
                        readers.setdefault(found, []).append(key)
            return stages[key]

        ends = [("out", component) for component in range(8)]
        for key in ends:
            stage(key)
        plans.append(
            [
                [
                    key
                    for key, at in stages.items()
                    if at == level
                    and (key in ends or any(stages[reader] > level for reader in readers[key]))
                ]
                for level in range(2)
            ]
        )
    return plans


def own_windows(wholes, row, row_shift, known):
    _, parts, cells_x, cells_y, cells_z = wholes.shape
    length = wholes.shape[0] * cells_y
    sub = lax.broadcasted_iota(jnp.int32, (cells_y, cells_z), 0)
    start = remainder(lax.axis_index("gy") * cells_y - row_shift[row] + length, length)
    read = tile_reader(wholes, start, length, -1, 3)
    for k in range(5):
        radial = row + k - 2
        if 0 <= radial < cells_x:
            for component in range(parts):
                before, main, after = read(component, radial)
                around = jnp.where(sub < 4, after, before)
                known["raw", k, component] = jnp.concatenate([main, around], axis=0)


def inner_call(whole, row_shift):
    _, _, cells_x, cells_y, cells_z = whole.shape
    plans = handed_on(cells_x)

    def body(row_shift, whole, out):
        at = 0
        for row in range(cells_x):
            known = {}
            own_windows(whole, row, row_shift, known)
            values = Row(known)
            for key in plans[row][0]:
                out[at] = values.get(*key)
                at += 1

    vmem = pl.BlockSpec(memory_space=pltpu.VMEM)
    total = sum(len(plan[0]) for plan in plans)
    return pl.pallas_call(
        body,
        out_shape=jax.ShapeDtypeStruct((total, 2 * cells_y, cells_z), jnp.float32),
        in_specs=[pl.BlockSpec(memory_space=pltpu.SMEM), vmem],
        out_specs=vmem,
        compiler_params=pltpu.CompilerParams(vmem_limit_bytes=32 * 1024 * 1024),
        cost_estimate=pl.CostEstimate(flops=10**7, bytes_accessed=10**6, transcendentals=10**5),
        name="inner",
    )(row_shift, whole)


def load_stage(plans, level, ref, known):
    at = 0
    for row, plan in enumerate(plans):
        for key in plan[level]:
            known[row][key] = ref[at]
            at += 1


def middle_call(inner, from_above, cells_x):
    plans = handed_on(cells_x)

    def body(inner, from_above, out):
        known = [{} for _ in range(cells_x)]
        load_stage(plans, 0, inner, known)
        unpack(from_above, high_windows(cells_x), known)
        at = 0
        for row in range(cells_x):
            values = Row(known[row])
            for key in plans[row][1]:
                out[at] = values.get(*key)
                at += 1

    vmem = pl.BlockSpec(memory_space=pltpu.VMEM)
    total = sum(len(plan[1]) for plan in plans)
    return pl.pallas_call(
        body,
        out_shape=jax.ShapeDtypeStruct((total,) + inner.shape[1:], jnp.float32),
        in_specs=[vmem] * 2,
        out_specs=vmem,
        compiler_params=pltpu.CompilerParams(vmem_limit_bytes=32 * 1024 * 1024),
        cost_estimate=pl.CostEstimate(flops=10**9, bytes_accessed=10**7, transcendentals=0),
        name="middle",
    )(inner, from_above)


def outer_call(inner, middle, from_below, cells_x, parts):
    cells_y, cells_z = inner.shape[1] // 2, inner.shape[2]
    plans = handed_on(cells_x)

    def body(inner, middle, from_below, out):
        known = [{} for _ in range(cells_x)]
        load_stage(plans, 0, inner, known)
        load_stage(plans, 1, middle, known)
        unpack(from_below, low_windows(cells_x), known)
        for row in range(cells_x):
            values = Row(known[row])
            for component in range(parts):
                out[component, row] = values.get("out", component)[0:cells_y]

    vmem = pl.BlockSpec(memory_space=pltpu.VMEM)
    return pl.pallas_call(
        body,
        out_shape=jax.ShapeDtypeStruct((parts, cells_x, cells_y, cells_z), jnp.float32),
        in_specs=[vmem] * 3,
        out_specs=vmem,
        compiler_params=pltpu.CompilerParams(vmem_limit_bytes=32 * 1024 * 1024),
        name="outer",
    )(inner, middle, from_below)


def on_device(fields, shear_offset, row_shift):
    count_x, count_y = lax.axis_size("gx"), lax.axis_size("gy")
    upward = [(i, (i + 1) % count_x) for i in range(count_x)]
    downward = [(target, source) for source, target in upward]

    def other_core(values):
        return lax.ppermute(values, "gy", [(i, i ^ 1) for i in range(count_y)])

    own = jnp.roll(fields, fields.shape[0] // 2, axis=0)
    meet = []
    for x in range(count_x):
        for y in range(count_y):
            other = (x + 1 if (x + y) % 2 == 0 else x - 1) % count_x
            meet.append((x * count_y + y, other * count_y + y))
    received = lax.ppermute(row_shift, ("gx", "gy"), meet)
    received, own = lax.optimization_barrier((received, own))
    swapped = other_core(received)
    near = [fields] + [
        lax.ppermute(fields, "gy", [(i, (i + step) % count_y) for i in range(count_y)])
        for step in range(2, count_y, 2)
    ]
    passed_on = list(near)
    far = [other_core(near[0]), other_core(near[1])]
    passed_on[2], received, swapped, _ = lax.optimization_barrier((near[2], received, swapped, far[1]))
    far.append(other_core(passed_on[2]))
    passed_on[3], _ = lax.optimization_barrier((near[3], passed_on[2]))
    far += [other_core(values) for values in passed_on[3:]]
    near[0] = own
    whole, to_below = windows_down_call(near, far, received, swapped, shear_offset)
    from_above = lax.ppermute(to_below, "gx", downward)
    to_above = windows_up_call(whole, received, swapped, shear_offset)
    from_below = lax.ppermute(to_above, "gx", upward)
    inner = inner_call(whole, row_shift)
    middle = middle_call(inner, from_above, fields.shape[1])
    return outer_call(inner, middle, from_below, fields.shape[1], fields.shape[0])


def solution(mesh):
    placed = (P(None, "gx", "gy", None), P(), P("gx"))
    return jax.shard_map(
        on_device, mesh=mesh, in_specs=placed, out_specs=P(None, "gx", "gy", None), check_vma=False
    )
```

```python
import functools
import jax
import jax.numpy as jnp
from jax import lax
from jax.experimental import pallas as pl
from jax.experimental.pallas import tpu as pltpu
from jax.sharding import PartitionSpec as P

time_step = 0.2
sound_squared = 1.0
shear_speed = 1.5
sweep_orders = ((0, 1, 2), (1, 2, 0), (2, 0, 1))


def remainder(value, by):
    return value & (by - 1) if by & (by - 1) == 0 else lax.rem(value, by)


def quotient(value, by):
    return value >> (by.bit_length() - 1) if by & (by - 1) == 0 else lax.div(value, by)


def minmod(first_diff, second_diff):
    return jnp.maximum(0.0, jnp.minimum(first_diff, second_diff)) + jnp.minimum(
        0.0, jnp.maximum(first_diff, second_diff)
    )


def shift(values, by, axis):
    return pltpu.roll(values, by % values.shape[axis], axis=axis)


def side_terms(state, normal_field):
    density, normal_vel, tang_one, tang_two, field_one, field_two, fraction = state
    normal_square = normal_field * normal_field
    tangent_square = field_one * field_one + field_two * field_two
    mass_flux = density * normal_vel
    dye = density * fraction
    fluxes = (
        mass_flux,
        mass_flux * normal_vel + sound_squared * density + 0.5 * (tangent_square - normal_square),
        mass_flux * tang_one - normal_field * field_one,
        mass_flux * tang_two - normal_field * field_two,
        normal_vel * field_one - tang_one * normal_field,
        normal_vel * field_two - tang_two * normal_field,
        dye * normal_vel,
    )
    conserved = (
        density,
        mass_flux,
        density * tang_one,
        density * tang_two,
        field_one,
        field_two,
        dye,
    )
    inverse = 1.0 / density
    normal_alfven = normal_square * inverse
    tangent_alfven = tangent_square * inverse
    apart = sound_squared - normal_alfven
    spread = (
        apart * apart
        + tangent_alfven * tangent_alfven
        + 2.0 * tangent_alfven * (sound_squared + normal_alfven)
    )
    fast_speed = jnp.sqrt(0.5 * (sound_squared + normal_alfven + tangent_alfven + jnp.sqrt(spread)))
    return (fluxes, conserved, normal_vel - fast_speed, normal_vel + fast_speed)


def hll_flux(left_side, right_side, normal_field):
    flux_left_all, cons_left_all, low_left, high_left = side_terms(left_side, normal_field)
    flux_right_all, cons_right_all, low_right, high_right = side_terms(right_side, normal_field)
    lower_speed = jnp.minimum(jnp.minimum(low_left, low_right), 0.0)
    upper_speed = jnp.maximum(jnp.maximum(high_left, high_right), 0.0)
    inverse_gap = 1.0 / (upper_speed - lower_speed)
    upper = upper_speed * inverse_gap
    lower = lower_speed * inverse_gap
    product = lower_speed * upper
    return tuple(
        upper * flux_left - lower * flux_right + product * (cons_right - cons_left)
        for flux_left, flux_right, cons_left, cons_right in zip(
            flux_left_all, flux_right_all, cons_left_all, cons_right_all
        )
    )


def low_windows(cells_x):
    return [(i, i + k) for i in range(cells_x) for k in (-2, -1) if i + k < 0]


def high_windows(cells_x):
    return [(i, i + k) for i in range(cells_x) for k in (1, 2) if i + k >= cells_x]


def tile_reader(source, start, length, first_tile, tiles):
    cells_y, cells_z = source.shape[3:]
    blocks = length // cells_y
    block = quotient(start, cells_y)
    turn = remainder(start, cells_y)
    inside = lax.broadcasted_iota(jnp.int32, (cells_y, cells_z), 0) < cells_y - turn
    places = [remainder(block + first_tile + k + blocks, blocks) for k in range(tiles + 1)]

    def read(component, row):
        turned = [pltpu.roll(source[place, component, row], cells_y - turn, axis=0) for place in places]
        return [jnp.where(inside, turned[k], turned[k + 1]) for k in range(tiles)]

    return read


class Row:
    def __init__(self, known):
        self.known = dict(known)

    def get(self, *key):
        if key not in self.known:
            getattr(self, "make_" + key[0])(*key[1:-1])
        return self.known[key]

    def all(self, *key):
        return tuple(self.get(*key, item) for item in range(7))

    def put(self, key, values):
        for item, value in enumerate(values):
            self.known[key + (item,)] = value

    def make_cell(self, k):
        raw = [self.get("raw", k, component) for component in range(8)]
        inverse = 1.0 / raw[0]
        self.put(
            ("cell", k),
            (
                raw[0],
                raw[1] * inverse,
                raw[2] * inverse,
                raw[3] * inverse,
                0.5 * (raw[6] + shift(raw[6], -1, 0)),
                0.5 * (raw[7] + shift(raw[7], -1, 1)),
                raw[4] * inverse,
            ),
        )

    def make_centre_x(self, k):
        self.put(("centre_x", k), [0.5 * (self.get("raw", k, 5) + self.get("raw", k + 1, 5))])

    def make_slope(self, k):
        three = [self.all("cell", k + step) for step in (-1, 0, 1)]
        self.put(("slope", k), [0.5 * minmod(h - b, a - h) for b, h, a in zip(*three)])

    def make_along_0(self, face):
        left = [w + s for w, s in zip(self.all("cell", face + 1), self.all("slope", face + 1))]
        right = [w - s for w, s in zip(self.all("cell", face + 2), self.all("slope", face + 2))]
        self.put(("along_0", face), hll_flux(left, right, self.get("raw", face + 2, 5)))

    def sweep(self, k, direction, axis):
        density, vel_x, vel_y, vel_z, centre_y, centre_z, fraction = self.all("cell", k)
        velocity = (vel_x, vel_y, vel_z)
        centres = (self.get("centre_x", k, 0), centre_y, centre_z)
        normal_axis, first_axis, second_axis = sweep_orders[direction]
        states = (
            density,
            velocity[normal_axis],
            velocity[first_axis],
            velocity[second_axis],
            centres[first_axis],
            centres[second_axis],
            fraction,
        )
        left, right = [], []
        for w in states:
            half = 0.5 * minmod(w - shift(w, 1, axis), shift(w, -1, axis) - w)
            left.append(shift(w + half, 1, axis))
            right.append(w - half)
        return hll_flux(left, right, self.get("raw", k, 5 + direction))

    def make_along_1(self, k):
        self.put(("along_1", k), self.sweep(k, 1, 0))

    def make_along_2(self, k):
        self.put(("along_2", k), self.sweep(k, 2, 1))

    def make_out(self):
        along_x = [self.all("along_0", face) for face in range(2)]
        along_y, along_z = self.all("along_1", 2), self.all("along_2", 2)
        edge_z = [
            0.25
            * (
                self.get("along_1", face + 2, 5)
                + self.get("along_1", face + 1, 5)
                - along_x[face][4]
                - shift(along_x[face][4], 1, 0)
            )
            for face in range(2)
        ]
        edge_y = [
            0.25
            * (
                along_x[face][5]
                + shift(along_x[face][5], 1, 1)
                - self.get("along_2", face + 2, 4)
                - self.get("along_2", face + 1, 4)
            )
            for face in range(2)
        ]
        edge_x = 0.25 * (
            along_z[5] + shift(along_z[5], 1, 0) - along_y[4] - shift(along_y[4], 1, 1)
        )
        own = [self.get("raw", 2, component) for component in range(8)]
        places = ((1, 2, 3), (3, 1, 2), (2, 3, 1))
        values = []
        for component in range(5):
            if component == 0:
                slots = (0, 0, 0)
            elif component == 4:
                slots = (6, 6, 6)
            else:
                slots = tuple(places[d][component - 1] for d in range(3))
            through_y, through_z = along_y[slots[1]], along_z[slots[2]]
            total = (
                along_x[1][slots[0]]
                - along_x[0][slots[0]]
                + shift(through_y, -1, 0)
                - through_y
                + shift(through_z, -1, 1)
                - through_z
            )
            values.append(own[component] - time_step * total)
        values.append(
            own[5]
            - time_step * (shift(edge_z[0], -1, 0) - edge_z[0])
            + time_step * (shift(edge_y[0], -1, 1) - edge_y[0])
        )
        values.append(
            own[6]
            - time_step * (shift(edge_x, -1, 1) - edge_x)
            + time_step * (edge_z[1] - edge_z[0])
        )
        values.append(
            own[7]
            - time_step * (edge_y[1] - edge_y[0])
            + time_step * (shift(edge_x, -1, 0) - edge_x)
        )
        self.put(("out",), values)


def message(wanted):
    mains, slots = [], []
    for row, radial in wanted:
        k = radial - row + 2
        if k in (1, 3):
            mains += [(row, "raw", k, component) for component in range(8)]
            slots += [[(row, "raw", k, component)] for component in (0, 1, 2, 5, 6, 7)]
        else:
            mains += [(row, "cell", k, item) for item in range(7)]
            slots += [[(row, "cell", k, item) for item in pair] for pair in ((0, 1), (2, 4), (5,))]
            if k == 4:
                mains.append((row, "raw", k, 5))
                slots.append([(row, "raw", k, 5)])
    return mains, slots


def message_tiles(wanted):
    mains, slots = message(wanted)
    return len(mains) + (len(slots) + 1) // 2


def pack(out, wanted, values):
    mains, slots = message(wanted)
    sub = lax.broadcasted_iota(jnp.int32, out.shape[1:], 0)
    rows = out.shape[1]
    for at, (row, *key) in enumerate(mains):
        out[at] = values[row].get(*key)[:rows]

    def slot(keys):
        around = [values[row].get(*key)[rows:] for row, *key in keys]
        first = around[0]
        tile = jnp.where(sub < 2, first, shift(first, 4, 0))
        if len(around) == 2:
            second = around[1]
            tile = jnp.where(sub == 1, shift(second, 1, 0), tile)
            tile = jnp.where(sub == 2, shift(second, 3, 0), tile)
        return tile

    for at in range(0, len(slots), 2):
        tile = slot(slots[at])
        if at + 1 < len(slots):
            tile = jnp.where(sub < 4, tile, shift(slot(slots[at + 1]), 4, 0))
        out[len(mains) + at // 2] = tile


def unpack(source, wanted, known):
    mains, slots = message(wanted)
    sub = lax.broadcasted_iota(jnp.int32, source.shape[1:], 0)
    edges = {}
    for at, keys in enumerate(slots):
        tile = source[len(mains) + at // 2]
        turned = shift(tile, 4, 0)
        one, two = (tile, turned) if at % 2 == 0 else (turned, tile)
        around = jnp.where(sub < 4, one, two)
        edges[keys[0]] = around
        if len(keys) == 2:
            edges[keys[1]] = jnp.where(sub < 4, shift(around, -1, 0), shift(around, 1, 0))
    for at, key in enumerate(mains):
        main = source[at]
        known[key[0]][key[1:]] = jnp.concatenate([main, edges.get(key, main)], axis=0)


def windows_call(near, far, received, swapped, offset):
    count = len(near)
    parts, cells_x, cells_y, cells_z = near[0].shape
    blocks = 2 * count
    length = blocks * cells_y
    lows, highs = low_windows(cells_x), high_windows(cells_x)

    def body(offset, received, swapped, *refs):
        ins, whole, outs = refs[:blocks], refs[blocks], refs[blocks + 1 :]
        place_x, place_y = lax.axis_index("gx"), lax.axis_index("gy")
        here = remainder(place_x + place_y, 2) == 0
        lane = lax.broadcasted_iota(jnp.int32, (1, cells_x), 1)
        one, other = (
            source[...].reshape(1, cells_x).astype(jnp.float32) for source in (received, swapped)
        )

        def scalars(values):
            return [
                jnp.sum(jnp.where(lane == i, values, 0.0)).astype(jnp.int32) for i in range(cells_x)
            ]

        above, below = scalars(jnp.where(here, one, other)), scalars(jnp.where(here, other, one))
        last = lax.axis_size("gx") - 1
        for side in range(2):
            for step in range(count):
                block = ins[side * count + step]
                place = remainder((place_y ^ side) - 2 * step + blocks, blocks)
                if side == 0 and step == 0:
                    whole[place, : parts // 2] = block[parts // 2 :]
                    whole[place, parts // 2 :] = block[: parts // 2]
                else:
                    whole[place] = block[...]
        sub = lax.broadcasted_iota(jnp.int32, (cells_y, cells_z), 0)
        for out, shift_by, wanted, end, sign, turn in (
            (outs[0], above, lows, last, 1, cells_x),
            (outs[1], below, highs, 0, -1, -cells_x),
        ):
            at_end = place_x == end
            away = jnp.where(at_end, sign * offset[0], 0)
            boost = jnp.where(at_end, sign * shear_speed, 0.0)
            known = {}
            for row, radial in wanted:
                start = remainder(place_y * cells_y - shift_by[row] + away + 2 * length, length)
                read = tile_reader(whole, start, length, -1, 3)
                raw = []
                for component in range(parts):
                    before, main, after = read(component, radial + turn)
                    raw.append(jnp.concatenate([main, jnp.where(sub < 4, after, before)], axis=0))
                raw[2] = raw[2] + boost * raw[0]
                for component in range(parts):
                    known.setdefault(row, {})["raw", radial - row + 2, component] = raw[component]
            pack(out, wanted, {row: Row(found) for row, found in known.items()})

    vmem = pl.BlockSpec(memory_space=pltpu.VMEM)
    smem = pl.BlockSpec(memory_space=pltpu.SMEM)
    return pl.pallas_call(
        body,
        out_shape=[jax.ShapeDtypeStruct((blocks, parts, cells_x, cells_y, cells_z), jnp.float32)]
        + [
            jax.ShapeDtypeStruct((message_tiles(wanted), cells_y, cells_z), jnp.float32)
            for wanted in (lows, highs)
        ],
        in_specs=[smem] + [vmem] * (2 + blocks),
        out_specs=[vmem] * 3,
        compiler_params=pltpu.CompilerParams(vmem_limit_bytes=32 * 1024 * 1024),
        name="windows",
    )(offset, received, swapped, *near, *far)


def reads(key):
    name, *rest = key
    if name == "out":
        found = [("raw", 2, component) for component in range(8)]
        found += [("along_0", face, item) for face in range(2) for item in range(7)]
        found += [(along, 2, item) for along in ("along_1", "along_2") for item in range(7)]
        return found + [(along, k, item) for k in (1, 3) for along, item in (("along_1", 5), ("along_2", 4))]
    if name == "cell":
        return [("raw", rest[0], component) for component in range(8)]
    if name == "centre_x":
        return [("raw", rest[0], 5), ("raw", rest[0] + 1, 5)]
    if name == "slope":
        return [("cell", rest[0] + step, rest[1]) for step in (-1, 0, 1)]
    if name == "along_0":
        cells = [rest[0] + 1, rest[0] + 2]
        found = [(of, k, item) for k in cells for of in ("cell", "slope") for item in range(7)]
        return found + [("raw", cells[1], 5)]
    found = [("cell", rest[0], item) for item in range(7)] + [("centre_x", rest[0], 0)]
    return found + [("raw", rest[0], {"along_1": 6, "along_2": 7}[name])]


def handed_on(cells_x):
    plans = []
    for row in range(cells_x):

        def stage_of_ghost(k):
            return 0 if 0 <= row + k - 2 < cells_x else 1 if row + k - 2 >= cells_x else 2

        stages, readers = {}, {}

        def stage(key):
            if key not in stages:
                given = key[0] == "raw" or (key[0] == "cell" and key[1] in (0, 4) and stage_of_ghost(key[1]))
                if given:
                    stages[key] = stage_of_ghost(key[1])
                else:
                    stages[key] = max(stage(found) for found in reads(key))
                    for found in reads(key):
                        readers.setdefault(found, []).append(key)
            return stages[key]

        ends = [("out", component) for component in range(8)]
        for key in ends:
            stage(key)
        plans.append(
            [
                [
                    key
                    for key, at in stages.items()
                    if at == level
                    and (key in ends or any(stages[reader] > level for reader in readers[key]))
                ]
                for level in range(2)
            ]
        )
    return plans


def own_windows(wholes, row, row_shift, known):
    _, parts, cells_x, cells_y, cells_z = wholes.shape
    length = wholes.shape[0] * cells_y
    sub = lax.broadcasted_iota(jnp.int32, (cells_y, cells_z), 0)
    start = remainder(lax.axis_index("gy") * cells_y - row_shift[row] + length, length)
    read = tile_reader(wholes, start, length, -1, 3)
    for k in range(5):
        radial = row + k - 2
        if 0 <= radial < cells_x:
            for component in range(parts):
                before, main, after = read(component, radial)
                around = jnp.where(sub < 4, after, before)
                known["raw", k, component] = jnp.concatenate([main, around], axis=0)


def inner_call(whole, row_shift):
    _, _, cells_x, cells_y, cells_z = whole.shape
    plans = handed_on(cells_x)

    def body(row_shift, whole, out):
        at = 0
        for row in range(cells_x):
            known = {}
            own_windows(whole, row, row_shift, known)
            values = Row(known)
            for key in plans[row][0]:
                out[at] = values.get(*key)
                at += 1

    vmem = pl.BlockSpec(memory_space=pltpu.VMEM)
    total = sum(len(plan[0]) for plan in plans)
    return pl.pallas_call(
        body,
        out_shape=jax.ShapeDtypeStruct((total, 2 * cells_y, cells_z), jnp.float32),
        in_specs=[pl.BlockSpec(memory_space=pltpu.SMEM), vmem],
        out_specs=vmem,
        compiler_params=pltpu.CompilerParams(vmem_limit_bytes=32 * 1024 * 1024),
        cost_estimate=pl.CostEstimate(flops=10**7, bytes_accessed=10**6, transcendentals=10**5),
        name="inner",
    )(row_shift, whole)


def load_stage(plans, level, ref, known):
    at = 0
    for row, plan in enumerate(plans):
        for key in plan[level]:
            known[row][key] = ref[at]
            at += 1


def middle_call(inner, from_above, cells_x):
    plans = handed_on(cells_x)

    def body(inner, from_above, out):
        known = [{} for _ in range(cells_x)]
        load_stage(plans, 0, inner, known)
        unpack(from_above, high_windows(cells_x), known)
        at = 0
        for row in range(cells_x):
            values = Row(known[row])
            for key in plans[row][1]:
                out[at] = values.get(*key)
                at += 1

    vmem = pl.BlockSpec(memory_space=pltpu.VMEM)
    total = sum(len(plan[1]) for plan in plans)
    return pl.pallas_call(
        body,
        out_shape=jax.ShapeDtypeStruct((total,) + inner.shape[1:], jnp.float32),
        in_specs=[vmem] * 2,
        out_specs=vmem,
        compiler_params=pltpu.CompilerParams(vmem_limit_bytes=32 * 1024 * 1024),
        cost_estimate=pl.CostEstimate(flops=10**6, bytes_accessed=10**6, transcendentals=10**4),
        name="middle",
    )(inner, from_above)


def outer_call(inner, middle, from_below, cells_x, parts):
    cells_y, cells_z = inner.shape[1] // 2, inner.shape[2]
    plans = handed_on(cells_x)

    def body(inner, middle, from_below, out):
        known = [{} for _ in range(cells_x)]
        load_stage(plans, 0, inner, known)
        load_stage(plans, 1, middle, known)
        unpack(from_below, low_windows(cells_x), known)
        for row in range(cells_x):
            values = Row(known[row])
            for component in range(parts):
                out[component, row] = values.get("out", component)[0:cells_y]

    vmem = pl.BlockSpec(memory_space=pltpu.VMEM)
    return pl.pallas_call(
        body,
        out_shape=jax.ShapeDtypeStruct((parts, cells_x, cells_y, cells_z), jnp.float32),
        in_specs=[vmem] * 3,
        out_specs=vmem,
        compiler_params=pltpu.CompilerParams(vmem_limit_bytes=32 * 1024 * 1024),
        name="outer",
    )(inner, middle, from_below)


def on_device(fields, shear_offset, row_shift):
    count_x, count_y = lax.axis_size("gx"), lax.axis_size("gy")
    upward = [(i, (i + 1) % count_x) for i in range(count_x)]
    downward = [(target, source) for source, target in upward]

    def other_core(values):
        return lax.ppermute(values, "gy", [(i, i ^ 1) for i in range(count_y)])

    own = jnp.roll(fields, fields.shape[0] // 2, axis=0)
    meet = []
    for x in range(count_x):
        for y in range(count_y):
            other = (x + 1 if (x + y) % 2 == 0 else x - 1) % count_x
            meet.append((x * count_y + y, other * count_y + y))
    received = lax.ppermute(row_shift, ("gx", "gy"), meet)
    received, own = lax.optimization_barrier((received, own))
    swapped = other_core(received)
    near = [fields] + [
        lax.ppermute(fields, "gy", [(i, (i + step) % count_y) for i in range(count_y)])
        for step in range(2, count_y, 2)
    ]
    passed_on = list(near)
    late, _ = lax.optimization_barrier((near[0], near[1]))
    far = [other_core(late), other_core(near[1])]
    passed_on[2], received, swapped, _ = lax.optimization_barrier((near[2], received, swapped, far[1]))
    far.append(other_core(passed_on[2]))
    passed_on[3], _ = lax.optimization_barrier((near[3], passed_on[2]))
    far += [other_core(values) for values in passed_on[3:]]
    near[0] = own
    whole, to_above, to_below = windows_call(near, far, received, swapped, shear_offset)
    from_below = lax.ppermute(to_above, "gx", upward)
    from_above = lax.ppermute(to_below, "gx", downward)
    inner = inner_call(whole, row_shift)
    middle = middle_call(inner, from_above, fields.shape[1])
    return outer_call(inner, middle, from_below, fields.shape[1], fields.shape[0])


def solution(mesh):
    placed = (P(None, "gx", "gy", None), P(), P("gx"))
    return jax.shard_map(
        on_device, mesh=mesh, in_specs=placed, out_specs=P(None, "gx", "gy", None), check_vma=False
    )
```
